32 devices in a mesh: group: 2 (over y), fsdp: 4 (over x, core), dp: 4 (over z).
Axes of the slice: x: 2, y: 2, z: 4, core: 2. Of those that a mesh axis runs over, the one named last changes fastest.
Arguments:
- activations: bfloat16 [12288, 8192], P(('group', 'fsdp', 'dp')), parts along dimension 0, may hold values from -6 to 6
- upstream: bfloat16 [12288, 1024], P(('group', 'fsdp', 'dp')), parts along dimension 0, may hold values from -6 to 6
- frozen: bfloat16 [8192, 1024], P('fsdp'), may hold values from -0.0625 to 0.0625
- deltas: bfloat16 [32, 128, 128], P(('group', 'fsdp')), parts along dimension 0, may hold values from -0.29882812 to 0.29882812
- block_rows: int32 [16], replicated, may hold values from 0 to 63, as said below
- block_cols: int32 [16], replicated, may hold values from 0 to 7
- block_slot: int32 [16], replicated, may hold values from 0 to 15, as said below
Outputs:
- grad_in: bfloat16 [12288, 8192], P(('group', 'fsdp', 'dp')), parts along dimension 0
- delta_grad: float32 [32, 128, 128], P(('group', 'fsdp')), parts along dimension 0
The draws below stay inside these ranges and needn't reach their ends.
There are 2 independent parts, one for each index of `group`. The reference program is written for one: setup_inputs(seed, part) draws one part's arguments, and reference() takes and returns one part's arrays. A program takes and returns all parts, laid end to end along the dimension named above; an argument that names none is the same for every part. Nothing has to cross between parts.
Inputs may be any that keep to these rules, and one draw needn't show every extreme that they name: The pairs (block_rows, block_cols) are distinct. `block_slot`: slots are distinct; at most 4 blocks have one owner slot // 4, and some owner holds exactly 4.
All inputs are finite; a program needn't handle non-finite values.
Results may differ from the reference program's by a relative error of at most 0.001.
Values may be sent and summed in bfloat16 or wider, within the bound.
No kernel may reach another device: no remote copies, remote signals or barrier semaphores. Data moves between devices by JAX's collectives and lax.ppermute only.
A program may use at most 128 MiB of HBM per device.

```python
import math
import jax
import jax.numpy as jnp
from jax import lax

D = 8192
KV = 1024
BLOCK = 128
NB = 16
SLOTS = 4
TOKENS = 6144
STORE = 16
RB = 64
CB = 8


def pattern_cells(key):
    return jax.random.permutation(jax.random.fold_in(key, 11), RB * CB)[:NB].astype(jnp.int32)


def draw_block_rows(key, part):
    cells = pattern_cells(key)
    return (cells // CB).astype(jnp.int32)


def draw_block_cols(key, part):
    cells = pattern_cells(key)
    return (cells % CB).astype(jnp.int32)


def draw_block_slot(key, part):
    key = jax.random.fold_in(key, 7)
    owners = STORE // SLOTS
    full_owner = jax.random.randint(jax.random.fold_in(key, 1), (), 0, owners).astype(jnp.int32)
    first_slots = full_owner * SLOTS + jnp.arange(SLOTS, dtype=jnp.int32)
    others = jax.random.permutation(jax.random.fold_in(key, 2), (owners - 1) * SLOTS)[:NB - SLOTS].astype(jnp.int32)
    other_owner = (full_owner + 1 + others // SLOTS) % owners
    rest_slots = other_owner * SLOTS + others % SLOTS
    return jnp.concatenate([first_slots, rest_slots]).astype(jnp.int32)


def block_levels(own_key, dims, cuts, smallest, top_value):
    def one(axis_at, shards_of):
        steps = jax.random.uniform(jax.random.fold_in(jax.random.fold_in(own_key, 6), axis_at), (shards_of,), jnp.float32, smallest / len(cuts), top_value / len(cuts))
        return jnp.repeat(jnp.exp(steps), dims[axis_at] // shards_of).reshape((-1,) + (1,) * (len(dims) - axis_at - 1))

    gain = one(*cuts[0])
    for cut in cuts[1:]:
        gain = gain * one(*cut)
    return gain


def centred(key, extent, width, most, cuts=(), held_as=jnp.bfloat16):
    factor_of = block_levels(key, extent, cuts, -0.22, 0.18) if cuts else 1.0
    array = jax.random.normal(key, extent, jnp.float32) * width * factor_of
    return jnp.minimum(jnp.maximum(array, -most), most).astype(held_as)


def setup_inputs(seed: int = 0, part: int = 0) -> dict:
    arg_keys = jax.random.split(jax.random.key(seed), 8)
    part_keys = jax.random.split(jax.random.fold_in(arg_keys[7], part), 8)
    activations = centred(part_keys[0], (TOKENS, D), 1.0, 6.0, ((0, 16),))
    upstream = centred(part_keys[1], (TOKENS, KV), 1.0, 6.0, ((0, 16),))
    frozen = centred(arg_keys[2], (D, KV), D ** -0.5, 0.0625, ((0, 4),))
    deltas = centred(part_keys[3], (STORE, BLOCK, BLOCK), 0.05, 0.29882812, ((0, 4),))
    block_rows = draw_block_rows(jax.random.fold_in(arg_keys[7], 71), part)
    block_cols = draw_block_cols(jax.random.fold_in(arg_keys[7], 71), part)
    block_slot = draw_block_slot(jax.random.fold_in(arg_keys[7], 71), part)
    return dict(activations=activations, upstream=upstream, frozen=frozen, deltas=deltas, block_rows=block_rows, block_cols=block_cols, block_slot=block_slot)


def reference(activations, upstream, frozen, deltas, block_rows, block_cols, block_slot):
    tok_rows = activations.shape[0]
    picked = jnp.take(deltas, block_slot, axis=0)
    dense_delta = jnp.zeros((D // BLOCK, BLOCK, KV // BLOCK, BLOCK), jnp.bfloat16)
    dense_delta = dense_delta.at[block_rows, :, block_cols, :].set(picked).reshape(D, KV)
    frozen_t = frozen.T
    delta_t = dense_delta.T

    def rows_grad(upstream_block):
        summed = jnp.dot(upstream_block, frozen_t, preferred_element_type=jnp.float32)
        summed = summed + jnp.dot(upstream_block, delta_t, preferred_element_type=jnp.float32)
        return summed.astype(jnp.bfloat16)
    grad_in = lax.map(rows_grad, upstream.reshape(8, tok_rows // 8, KV)).reshape(tok_rows, D)
    act_blocks = jnp.take(activations.reshape(tok_rows, D // BLOCK, BLOCK), block_rows, axis=1)
    up_blocks = jnp.take(upstream.reshape(tok_rows, KV // BLOCK, BLOCK), block_cols, axis=1)
    block_sum = jnp.einsum('tbi,tbj->bij', act_blocks.astype(jnp.float32), up_blocks.astype(jnp.float32))
    normalizer = 1.0 / math.sqrt(tok_rows)
    delta_grad = jnp.zeros((STORE, BLOCK, BLOCK), jnp.float32).at[block_slot].set(block_sum * normalizer)
    return (grad_in, delta_grad)
```

```python
import functools
import math

import jax
import jax.numpy as jnp
from jax import lax
from jax.experimental import pallas as pl
from jax.experimental.pallas import tpu as pltpu
from jax.sharding import PartitionSpec as P

BLOCK = 128
VMEM_BYTES = 40 * 1024 * 1024
SMEM_SPEC = pl.BlockSpec(memory_space=pltpu.SMEM)
ANY_SPEC = pl.BlockSpec(memory_space=pl.ANY)
VMEM_SPEC = pl.BlockSpec(memory_space=pltpu.VMEM)


def dot_nt(left, right):
    return lax.dot_general(
        left, right, (((1,), (1,)), ((), ())), preferred_element_type=jnp.float32
    )


def dot_tn(left, right):
    return lax.dot_general(
        left, right, (((0,), (0,)), ((), ())), preferred_element_type=jnp.float32
    )


def grad_kernel(place, outs, where_ref, rows_ref, cols_ref, slots_ref, act_ref, up_ref, *refs):
    out_refs, (act_buf, up_buf, act_sem, up_sem) = refs[:outs], refs[outs:]
    nb = rows_ref.shape[0]
    up_copy = pltpu.make_async_copy(up_ref, up_buf, up_sem)
    up_copy.start()

    def act_copy(b):
        column = pl.multiple_of(rows_ref[b] * BLOCK, BLOCK)
        return pltpu.make_async_copy(
            act_ref.at[:, pl.ds(column, BLOCK)], act_buf.at[b], act_sem.at[b]
        )

    for b in range(nb):
        act_copy(b).start()
    for ref in out_refs:
        ref[...] = jnp.zeros_like(ref)
    up_copy.wait()
    for b in range(nb):
        act_copy(b).wait()
        column = pl.multiple_of(cols_ref[b] * BLOCK, BLOCK)
        term = dot_tn(act_buf[b], up_buf[:, pl.ds(column, BLOCK)])
        which, index = place(where_ref, slots_ref[b])
        for n, ref in enumerate(out_refs):

            @pl.when(which == n)
            def _():
                ref[index] = term


def block_grads(place, shapes, where, rows, cols, slots, act, up):
    nb = rows.shape[0]
    return pl.pallas_call(
        functools.partial(grad_kernel, place, len(shapes)),
        out_shape=[jax.ShapeDtypeStruct((n, BLOCK, BLOCK), jnp.float32) for n in shapes],
        in_specs=[SMEM_SPEC] * 4 + [ANY_SPEC] * 2,
        out_specs=[VMEM_SPEC] * len(shapes),
        scratch_shapes=[
            pltpu.VMEM((nb, act.shape[0], BLOCK), act.dtype),
            pltpu.VMEM(up.shape, up.dtype),
            pltpu.SemaphoreType.DMA((nb,)),
            pltpu.SemaphoreType.DMA,
        ],
        compiler_params=pltpu.CompilerParams(vmem_limit_bytes=VMEM_BYTES),
        cost_estimate=pl.CostEstimate(
            flops=2 * nb * act.shape[0] * BLOCK * BLOCK,
            bytes_accessed=8 * nb * act.shape[0] * BLOCK,
            transcendentals=0,
        ),
        name="block_grads",
    )(where, rows, cols, slots, act, up)


def rows_kernel(
    units, tile, row_blocks, delta_at, n_w, n_d, aliased,
    where_ref, rows_ref, cols_ref, slots_ref, up_ref, *refs,
):
    w_refs, refs = refs[:n_w], refs[n_w:]
    d_refs, refs = refs[:n_d], refs[n_d:]
    if aliased:
        refs = refs[1:]
    out_ref, up_buf, w_buf, d_buf, acc, o_buf, table, mask, up_sem, w_sem, d_sem, o_sem = refs
    nb = rows_ref.shape[0]
    n_units = len(units)
    per = d_buf.shape[0] // n_d

    up_copy = pltpu.make_async_copy(up_ref, up_buf, up_sem)
    up_copy.start()
    for u, (w, first, _) in enumerate(units):
        pltpu.make_async_copy(
            w_refs[w].at[pl.ds(first, BLOCK)], w_buf.at[pl.ds(u * BLOCK, BLOCK)], w_sem.at[u]
        ).start()
    d_copies = [
        pltpu.make_async_copy(ref, d_buf.at[pl.ds(n * per, per)], d_sem.at[n])
        for n, ref in enumerate(d_refs)
    ]
    for copy in d_copies:
        copy.start()
    for u, (_, _, column) in enumerate(units):
        table[u] = column(where_ref)

    def clear(r, carry):
        mask[r] = 0
        return carry

    lax.fori_loop(0, row_blocks, clear, 0)
    for b in range(nb):
        r = rows_ref[b]
        mask[r] = mask[r] | (1 << b)
    up_copy.wait()
    for copy in d_copies:
        copy.wait()

    def out_copy(u):
        column = pl.multiple_of(table[u] * BLOCK, BLOCK)
        return pltpu.make_async_copy(
            o_buf.at[u], out_ref.at[:, pl.ds(column, BLOCK)], o_sem.at[u]
        )

    def step(t, width):
        for h in range(width):
            pltpu.make_async_copy(
                w_refs[0].at[pl.ds(0, BLOCK)],
                w_buf.at[pl.ds((t + h) * BLOCK, BLOCK)],
                w_sem.at[t + h],
            ).wait()
        size = width * BLOCK
        start = t * BLOCK if isinstance(t, int) else pl.multiple_of(t * BLOCK, BLOCK)
        acc[:, :size] = dot_nt(up_buf[...], w_buf[pl.ds(start, size)])
        for h in range(width):
            bits = mask[table[t + h]]

            @pl.when(bits != 0)
            def _():
                def one(b, carry):
                    @pl.when(((bits >> b) & 1) != 0)
                    def _():
                        column = pl.multiple_of(cols_ref[b] * BLOCK, BLOCK)
                        delta = d_buf[delta_at(where_ref, slots_ref[b])]
                        acc[:, h * BLOCK : (h + 1) * BLOCK] += dot_nt(
                            up_buf[:, pl.ds(column, BLOCK)], delta
                        )

                    return carry

                lax.fori_loop(0, nb, one, 0)

            o_buf[t + h] = acc[:, h * BLOCK : (h + 1) * BLOCK].astype(o_buf.dtype)
            out_copy(t + h).start()

    whole = n_units // tile
    if whole > 1:

        def body(k, carry):
            step(k * tile, tile)
            return carry

        lax.fori_loop(0, whole, body, 0)
    elif whole == 1:
        step(0, tile)
    if n_units % tile:
        step(whole * tile, n_units % tile)

    def finish(u, carry):
        out_copy(u).wait()
        return carry

    lax.fori_loop(0, n_units, finish, 0)


def rows_grad(units, weights, where, rows, cols, slots, up, deltas, delta_at, width, out=None, tile=4):
    n_units = len(units)
    tile = min(tile, n_units)
    tokens, depth = up.shape
    stored = sum(d.shape[0] for d in deltas)
    operands = [where, rows, cols, slots, up, *weights, *deltas]
    if out is not None:
        operands.append(out)
    return pl.pallas_call(
        functools.partial(
            rows_kernel, units, tile, width // BLOCK, delta_at, len(weights), len(deltas),
            out is not None,
        ),
        out_shape=jax.ShapeDtypeStruct((tokens, width), up.dtype),
        in_specs=[SMEM_SPEC] * 4 + [ANY_SPEC] * (len(operands) - 4),
        out_specs=ANY_SPEC,
        input_output_aliases={} if out is None else {len(operands) - 1: 0},
        scratch_shapes=[
            pltpu.VMEM((tokens, depth), up.dtype),
            pltpu.VMEM((n_units * BLOCK, depth), up.dtype),
            pltpu.VMEM((stored, BLOCK, BLOCK), up.dtype),
            pltpu.VMEM((tokens, tile * BLOCK), jnp.float32),
            pltpu.VMEM((n_units, tokens, BLOCK), up.dtype),
            pltpu.SMEM((n_units,), jnp.int32),
            pltpu.SMEM((width // BLOCK,), jnp.int32),
            pltpu.SemaphoreType.DMA,
            pltpu.SemaphoreType.DMA((n_units,)),
            pltpu.SemaphoreType.DMA((len(deltas),)),
            pltpu.SemaphoreType.DMA((n_units,)),
        ],
        compiler_params=pltpu.CompilerParams(vmem_limit_bytes=VMEM_BYTES),
        cost_estimate=pl.CostEstimate(
            flops=2 * tokens * depth * n_units * BLOCK,
            bytes_accessed=2 * n_units * BLOCK * (depth + tokens),
            transcendentals=0,
        ),
        name="rows_grad",
    )(*operands)


def gathered(activations, upstream, frozen, deltas, block_rows, block_cols, block_slot):
    local_slots = deltas.shape[0]
    local_rows = frozen.shape[0]
    n = lax.axis_size("fsdp")
    width = activations.shape[1]
    where = jnp.zeros((2,), jnp.int32)
    pattern = (where, block_rows, block_cols, block_slot)

    (partial,) = block_grads(
        lambda where_ref, slot: (0, slot), [n * local_slots], *pattern, activations, upstream
    )
    mine = lax.psum_scatter(partial, "fsdp", scatter_dimension=0, tiled=True)
    totals = lax.psum(mine, "dp")

    all_deltas = lax.all_gather(deltas, "fsdp", axis=0, tiled=True)
    weight = lax.all_gather(frozen, "fsdp", axis=0, tiled=True)
    out = None
    for first in range(0, width, 2048):
        units = [
            (0, first + k * BLOCK, lambda where_ref, c=first // BLOCK + k: c)
            for k in range(min(2048, width - first) // BLOCK)
        ]
        out = rows_grad(
            units, [weight], *pattern, upstream, [all_deltas],
            lambda where_ref, slot: slot, width, out,
        )
    return out, totals


def relayed(activations, upstream, frozen, deltas, block_rows, block_cols, block_slot):
    local_slots = deltas.shape[0]
    quarter = frozen.shape[0]
    depth = frozen.shape[1]
    width = activations.shape[1]
    f = lax.axis_index("fsdp")
    y = lax.axis_index("group")
    z = lax.axis_index("dp")
    n_dp = lax.axis_size("dp")
    even = z % 2
    cell = 2 * y + even
    where = jnp.stack([f, cell]).astype(jnp.int32)
    pattern = (where, block_rows, block_cols, block_slot)

    def over_core(a):
        return lax.ppermute(a, "fsdp", [(k, k ^ 1) for k in range(4)])

    def over_x(a):
        return lax.ppermute(a, "fsdp", [(k, k ^ 2) for k in range(4)])

    def over_y(a):
        return lax.ppermute(a, "group", [(k, k ^ 1) for k in range(2)])

    def over_z(a, step=1):
        return lax.ppermute(a, "dp", [(k, k ^ step) for k in range(n_dp)])

    part = quarter // 4
    sizes = (part // 4, part // 4, part // 2)
    offs = (0, sizes[0], sizes[0] + sizes[1])

    def own_rows(flip, k):
        return lax.dynamic_slice_in_dim(frozen, (cell ^ flip) * part + offs[k], sizes[k], 0)

    sib = over_core(frozen)
    x0 = over_x(own_rows(0, 0))
    dx = over_x(deltas)
    x1 = over_x(own_rows(0, 1))
    x2 = over_x(own_rows(0, 2))
    x3 = over_x(own_rows(3, 2))
    y0, z0 = over_y(x0), over_z(x0)
    y1, z1 = over_y(x1), over_z(x1)
    yd, zd = over_y(z0), over_z(y1)
    y2, z2 = over_y(x2), over_z(x2)
    dc = over_core(deltas)
    dxc = over_core(dx)
    all_deltas = [deltas, dc, dx, dxc]

    def delta_at(where_ref, slot):
        return ((slot // local_slots) ^ where_ref[0]) * local_slots + slot % local_slots

    def units_of(pieces):
        units = []
        for w, (a, flip_f, flip_cell, first) in enumerate(pieces):
            for k in range(a.shape[0] // BLOCK):
                def column(where_ref, flip_f=flip_f, flip_cell=flip_cell, at=first + k * BLOCK):
                    base = (where_ref[0] ^ flip_f) * (quarter // BLOCK)
                    if flip_cell is not None:
                        base = base + (where_ref[1] ^ flip_cell) * (part // BLOCK)
                    return base + at // BLOCK
                units.append((w, k * BLOCK, column))
        return units

    def grad_of(pieces, out):
        return rows_grad(
            units_of(pieces), [p[0] for p in pieces], *pattern, upstream, all_deltas,
            delta_at, width, out,
        )

    def both(a, flip_cell, first):
        return [(a, 2, flip_cell, first), (over_core(a), 3, flip_cell, first)]

    half = local_slots // 2

    def place(where_ref, slot):
        rel = (slot // local_slots) ^ where_ref[0]
        at = slot % local_slots
        index = (rel // 2) * local_slots + ((at // half) ^ (where_ref[1] % 2)) * half + at % half
        return rel % 2, index

    keep, send = block_grads(
        place, [2 * local_slots, 2 * local_slots], *pattern, activations, upstream
    )
    summed = keep + over_core(send)
    owned = summed[:local_slots] + over_x(summed[local_slots:])
    mine = owned[:half] + over_z(owned[half:])
    mine = mine + over_z(mine, 2)
    other = over_z(mine)
    normalizer = 1.0 / math.sqrt(upstream.shape[0] * lax.axis_size("fsdp") * n_dp)
    totals = jnp.where(
        even == 0,
        jnp.concatenate([mine, other], axis=0),
        jnp.concatenate([other, mine], axis=0),
    ) * normalizer

    out = grad_of([(frozen, 0, None, 0)], None)
    out = grad_of([(sib, 1, None, 0)], out)
    out = grad_of(
        both(x0, 0, offs[0]) + both(x1, 0, offs[1]) + both(y0, 2, offs[0]) + both(z0, 1, offs[0]), out
    )
    out = grad_of(
        both(y1, 2, offs[1]) + both(z1, 1, offs[1]) + both(yd, 3, offs[0]) + both(zd, 3, offs[1])
        + both(x2, 0, offs[2]), out,
    )
    out = grad_of(both(x3, 3, offs[2]) + both(y2, 2, offs[2]) + both(z2, 1, offs[2]), out)
    return out, totals


def normalized(activations, upstream, frozen, deltas, block_rows, block_cols, block_slot):
    out, totals = gathered(
        activations, upstream, frozen, deltas, block_rows, block_cols, block_slot
    )
    tokens = upstream.shape[0] * lax.axis_size("fsdp") * lax.axis_size("dp")
    return out, totals * (1.0 / math.sqrt(tokens))


def solution(mesh):
    sizes = dict(mesh.shape)
    cells = sizes["fsdp"] == 4 and sizes["group"] == 2 and sizes["dp"] == 4
    return jax.shard_map(
        relayed if cells else normalized,
        mesh=mesh,
        in_specs=(
            P(("group", "fsdp", "dp"), None),
            P(("group", "fsdp", "dp"), None),
            P("fsdp", None),
            P(("group", "fsdp"), None, None),
            P(),
            P(),
            P(),
        ),
        out_specs=(P(("group", "fsdp", "dp"), None), P(("group", "fsdp"), None, None)),
        check_vma=False,
    )
```

```python
import functools
import math

import jax
import jax.numpy as jnp
from jax import lax
from jax.experimental import pallas as pl
from jax.experimental.pallas import tpu as pltpu
from jax.sharding import PartitionSpec as P

BLOCK = 128
VMEM_BYTES = 60 * 1024 * 1024
ANY_SPEC = pl.BlockSpec(memory_space=pl.ANY)
HBM_SPEC = pl.BlockSpec(memory_space=pltpu.HBM)
COST = pl.CostEstimate(flops=1024, bytes_accessed=1024, transcendentals=0)
VMEM_SPEC = pl.BlockSpec(memory_space=pltpu.VMEM)


def dot_nt(left, right):
    return lax.dot_general(
        left, right, (((1,), (1,)), ((), ())), preferred_element_type=jnp.float32
    )


def dot_tn(left, right):
    return lax.dot_general(
        left, right, (((0,), (0,)), ((), ())), preferred_element_type=jnp.float32
    )


def after(value, *earlier):
    return lax.optimization_barrier((value, *earlier))[0]


def grad_kernel(place, outs, cuts, rows_hbm, cols_hbm, slots_hbm, act_ref, up_ref, *refs):
    refs = list(refs)
    w_ref = refs.pop(0) if cuts else None
    out_refs, refs = refs[:outs], refs[outs:]
    cut_refs, refs = refs[: len(cuts)], refs[len(cuts) :]
    rows_ref, cols_ref, slots_ref, act_buf, up_buf, act_sem, up_sem, i_sem, c_sem = refs
    nb = rows_ref.shape[0]
    index_copies = [
        pltpu.make_async_copy(src, dst, i_sem.at[n])
        for n, (src, dst) in enumerate(
            [(rows_hbm, rows_ref), (cols_hbm, cols_ref), (slots_hbm, slots_ref)]
        )
    ]
    for copy in index_copies:
        copy.start()
    up_copy = pltpu.make_async_copy(up_ref, up_buf, up_sem)
    up_copy.start()

    def act_copy(b):
        column = pl.multiple_of(rows_ref[b] * BLOCK, BLOCK)
        return pltpu.make_async_copy(
            act_ref.at[:, pl.ds(column, BLOCK)], act_buf.at[b], act_sem.at[b]
        )

    for copy in index_copies:
        copy.wait()
    for b in range(nb):
        act_copy(b).start()
    cut_copies = [
        pltpu.make_async_copy(
            w_ref.at[pl.ds(pl.multiple_of(first(), BLOCK), ref.shape[0])], ref, c_sem.at[n]
        )
        for n, ((first, _), ref) in enumerate(zip(cuts, cut_refs))
    ]
    for copy in cut_copies:
        copy.start()
    for ref in out_refs:
        ref[...] = jnp.zeros_like(ref)
    up_copy.wait()
    for b in range(nb):
        act_copy(b).wait()
        column = pl.multiple_of(cols_ref[b] * BLOCK, BLOCK)
        term = dot_tn(act_buf[b], up_buf[:, pl.ds(column, BLOCK)])
        which, index = place(slots_ref[b])
        for n, ref in enumerate(out_refs):

            @pl.when(which == n)
            def _():
                ref[index] = term

    for copy in cut_copies:
        copy.wait()


def block_grads(place, shapes, rows, cols, slots, act, up, weight=None, cuts=()):
    nb = rows.shape[0]
    return pl.pallas_call(
        functools.partial(grad_kernel, place, len(shapes), cuts),
        out_shape=[jax.ShapeDtypeStruct((n, BLOCK, BLOCK), jnp.float32) for n in shapes]
        + [jax.ShapeDtypeStruct((n, weight.shape[1]), weight.dtype) for _, n in cuts],
        in_specs=[HBM_SPEC] * (6 if cuts else 5),
        out_specs=[VMEM_SPEC] * (len(shapes) + len(cuts)),
        scratch_shapes=[
            pltpu.SMEM((nb,), jnp.int32),
            pltpu.SMEM((nb,), jnp.int32),
            pltpu.SMEM((nb,), jnp.int32),
            pltpu.VMEM((nb, act.shape[0], BLOCK), act.dtype),
            pltpu.VMEM(up.shape, up.dtype),
            pltpu.SemaphoreType.DMA((nb,)),
            pltpu.SemaphoreType.DMA,
            pltpu.SemaphoreType.DMA((3,)),
            pltpu.SemaphoreType.DMA((max(1, len(cuts)),)),
        ],
        compiler_params=pltpu.CompilerParams(vmem_limit_bytes=VMEM_BYTES),
        cost_estimate=COST,
        name="block_grads",
    )(rows, cols, slots, act, up, *([weight] if cuts else []))


def rows_kernel(
    units, moves, tile, row_blocks, delta_at, n_up, n_w, n_d, n_m, n_alias, other_first, *refs
):
    refs = list(refs)

    def take(n):
        taken = refs[:n]
        del refs[:n]
        return taken

    rows_hbm, cols_hbm, slots_hbm = take(3)
    up_refs, w_refs, d_refs, m_refs = take(n_up), take(n_w), take(n_d), take(n_m)
    take(n_alias)
    (out_ref,) = take(1)
    other_ref = take(1)[0] if n_up > 1 else None
    rows_ref, cols_ref, slots_ref, up_buf, w_buf, d_buf, acc, o_buf, m_buf = take(9)
    table, head, after_it, i_sem, up_sem, w_sem, d_sem, o_sem, m_sem = take(9)
    nb = rows_ref.shape[0]
    n_units = len(units)
    per = d_buf.shape[0] // n_d
    tokens = up_buf.shape[0] // n_up

    index_copies = [
        pltpu.make_async_copy(src, dst, i_sem.at[n])
        for n, (src, dst) in enumerate(
            [(rows_hbm, rows_ref), (cols_hbm, cols_ref), (slots_hbm, slots_ref)]
        )
    ]
    for copy in index_copies:
        copy.start()
    up_copies = [
        pltpu.make_async_copy(ref, up_buf.at[pl.ds(n * tokens, tokens)], up_sem.at[n])
        for n, ref in enumerate(up_refs)
    ]
    for copy in up_copies:
        copy.start()
    for u, (w, first, _) in enumerate(units):
        pltpu.make_async_copy(
            w_refs[w].at[pl.ds(first, BLOCK)], w_buf.at[pl.ds(u * BLOCK, BLOCK)], w_sem.at[u]
        ).start()
    d_copies = [
        pltpu.make_async_copy(ref, d_buf.at[pl.ds(n * per, per)], d_sem.at[n])
        for n, ref in enumerate(d_refs)
    ]
    for copy in d_copies:
        copy.start()
    m_in = [
        pltpu.make_async_copy(
            m_refs[m].at[:, pl.ds(first, BLOCK)], m_buf.at[n], m_sem.at[0, n]
        )
        for n, (m, first, _) in enumerate(moves)
    ]
    m_out = [
        pltpu.make_async_copy(
            m_buf.at[n],
            out_ref.at[:, pl.ds(pl.multiple_of(column() * BLOCK, BLOCK), BLOCK)],
            m_sem.at[1, n],
        )
        for n, (_, _, column) in enumerate(moves)
    ]
    for copy in m_in:
        copy.start()
    for u, (_, _, column) in enumerate(units):
        table[u] = column()
    for r in range(row_blocks):
        head[r] = -1
    for copy in index_copies:
        copy.wait()
    for b in range(nb):
        r = rows_ref[b]
        after_it[b] = head[r]
        head[r] = b
    for copy in up_copies:
        copy.wait()
    for copy in d_copies:
        copy.wait()

    def out_copies(u):
        column = pl.multiple_of(table[u] * BLOCK, BLOCK)
        copies = [
            pltpu.make_async_copy(
                o_buf.at[u, pl.ds(0, tokens)], out_ref.at[:, pl.ds(column, BLOCK)], o_sem.at[0, u]
            )
        ]
        if other_ref is not None:
            at = other_first + u * BLOCK
            at = at if isinstance(u, int) else pl.multiple_of(at, BLOCK)
            copies.append(
                pltpu.make_async_copy(
                    o_buf.at[u, pl.ds(tokens, tokens)],
                    other_ref.at[:, pl.ds(at, BLOCK)],
                    o_sem.at[1, u],
                )
            )
        return copies

    def step(t, width):
        for h in range(width):
            pltpu.make_async_copy(
                w_refs[0].at[pl.ds(0, BLOCK)],
                w_buf.at[pl.ds((t + h) * BLOCK, BLOCK)],
                w_sem.at[t + h],
            ).wait()
        size = width * BLOCK
        start = t * BLOCK if isinstance(t, int) else pl.multiple_of(t * BLOCK, BLOCK)
        acc[:, :size] = dot_nt(up_buf[...], w_buf[pl.ds(start, size)])
        for h in range(width):

            def add(b):
                column = pl.multiple_of(cols_ref[b] * BLOCK, BLOCK)
                delta = d_buf[delta_at(slots_ref[b])]
                acc[:, h * BLOCK : (h + 1) * BLOCK] += dot_nt(
                    up_buf[:, pl.ds(column, BLOCK)], delta
                )
                return after_it[b]

            lax.while_loop(lambda b: b >= 0, add, head[table[t + h]])
            o_buf[t + h] = acc[:, h * BLOCK : (h + 1) * BLOCK].astype(o_buf.dtype)
            for copy in out_copies(t + h):
                copy.start()

    whole = n_units // tile
    if whole > 1:

        def body(k, carry):
            step(k * tile, tile)
            return carry

        lax.fori_loop(0, whole, body, 0)
    elif whole == 1:
        step(0, tile)
    if n_units % tile:
        step(whole * tile, n_units % tile)

    for copy in m_in:
        copy.wait()
    for copy in m_out:
        copy.start()
    for copy in m_out:
        copy.wait()
    for u in range(n_units):
        for copy in out_copies(u):
            copy.wait()


def rows_grad(
    units, weights, rows, cols, slots, ups, deltas, delta_at, width, out=None, moves=(), moved=(), tile=4,
    other=None, other_units=None, other_first=0,
):
    n_units = len(units)
    tile = min(tile, n_units)
    tokens, depth = ups[0].shape
    dtype = ups[0].dtype
    stored = sum(d.shape[0] for d in deltas)
    nb = rows.shape[0]
    operands = [rows, cols, slots, *ups, *weights, *deltas, *moved]
    specs = [HBM_SPEC] * 3 + [ANY_SPEC] * (len(operands) - 3)
    alias = {}
    for n, held in enumerate([out, other]):
        if held is not None:
            alias[len(operands)] = n
            operands.append(held)
            specs.append(HBM_SPEC)
    shapes = [jax.ShapeDtypeStruct((tokens, width), dtype)]
    if len(ups) > 1:
        shapes.append(
            jax.ShapeDtypeStruct((tokens, (other_units or n_units) * BLOCK), dtype)
        )
    return pl.pallas_call(
        functools.partial(
            rows_kernel, units, moves, tile, width // BLOCK, delta_at, len(ups), len(weights),
            len(deltas), len(moved), len(alias), other_first,
        ),
        out_shape=shapes,
        in_specs=specs,
        out_specs=[HBM_SPEC] * len(shapes),
        input_output_aliases=alias,
        scratch_shapes=[
            pltpu.SMEM((nb,), jnp.int32),
            pltpu.SMEM((nb,), jnp.int32),
            pltpu.SMEM((nb,), jnp.int32),
            pltpu.VMEM((len(ups) * tokens, depth), dtype),
            pltpu.VMEM((n_units * BLOCK, depth), dtype),
            pltpu.VMEM((stored, BLOCK, BLOCK), dtype),
            pltpu.VMEM((len(ups) * tokens, tile * BLOCK), jnp.float32),
            pltpu.VMEM((n_units, len(ups) * tokens, BLOCK), dtype),
            pltpu.VMEM((max(1, len(moves)), tokens, BLOCK), dtype),
            pltpu.SMEM((n_units,), jnp.int32),
            pltpu.SMEM((width // BLOCK,), jnp.int32),
            pltpu.SMEM((nb,), jnp.int32),
            pltpu.SemaphoreType.DMA((3,)),
            pltpu.SemaphoreType.DMA((len(ups),)),
            pltpu.SemaphoreType.DMA((n_units,)),
            pltpu.SemaphoreType.DMA((len(deltas),)),
            pltpu.SemaphoreType.DMA((len(ups), n_units)),
            pltpu.SemaphoreType.DMA((2, max(1, len(moves)))),
        ],
        compiler_params=pltpu.CompilerParams(vmem_limit_bytes=VMEM_BYTES),
        cost_estimate=COST,
        name="rows_grad",
    )(*operands)


def gathered(activations, upstream, frozen, deltas, block_rows, block_cols, block_slot):
    local_slots = deltas.shape[0]
    n = lax.axis_size("fsdp")
    width = activations.shape[1]
    pattern = (block_rows, block_cols, block_slot)

    (partial,) = block_grads(
        lambda slot: (0, slot), [n * local_slots], *pattern, activations, upstream
    )
    mine = lax.psum_scatter(partial, "fsdp", scatter_dimension=0, tiled=True)
    totals = lax.psum(mine, "dp")

    all_deltas = lax.all_gather(deltas, "fsdp", axis=0, tiled=True)
    weight = lax.all_gather(frozen, "fsdp", axis=0, tiled=True)
    out = None
    for first in range(0, width, 2048):
        units = [
            (0, first + k * BLOCK, lambda c=first // BLOCK + k: c)
            for k in range(min(2048, width - first) // BLOCK)
        ]
        (out,) = rows_grad(
            units, [weight], *pattern, [upstream], [all_deltas], lambda slot: slot, width, out
        )
    tokens = upstream.shape[0] * n * lax.axis_size("dp")
    return out, totals * (1.0 / math.sqrt(tokens))


def relayed(activations, upstream, frozen, deltas, block_rows, block_cols, block_slot):
    local_slots = deltas.shape[0]
    quarter = frozen.shape[0]
    width = activations.shape[1]
    n_dp = lax.axis_size("dp")
    pattern = (block_rows, block_cols, block_slot)

    def my_f():
        return lax.axis_index("fsdp")

    def my_cell():
        return 2 * lax.axis_index("group") + lax.axis_index("dp") % 2

    def over_core(a):
        return lax.ppermute(a, "fsdp", [(k, k ^ 1) for k in range(4)])

    def over_x(a):
        return lax.ppermute(a, "fsdp", [(k, k ^ 2) for k in range(4)])

    def over_y(a):
        return lax.ppermute(a, "group", [(k, k ^ 1) for k in range(2)])

    def over_z(a, step=1):
        return lax.ppermute(a, "dp", [(k, k ^ step) for k in range(n_dp)])

    part = quarter // 4
    sizes = (part // 4, part // 4, part // 2)
    offs = (0, sizes[0], sizes[0] + sizes[1])

    def own_rows(flip, k):
        first = (my_cell() ^ flip) * part + offs[k]
        return lax.dynamic_slice_in_dim(frozen, first, sizes[k], 0)

    def delta_at(slot):
        return ((slot // local_slots) ^ my_f()) * local_slots + slot % local_slots

    def column_of(flip_f, flip_cell, at):
        def column():
            base = (my_f() ^ flip_f) * (quarter // BLOCK) + at // BLOCK
            if flip_cell is not None:
                base = base + (my_cell() ^ flip_cell) * (part // BLOCK)
            return base

        return column

    def units_of(pieces):
        return [
            (w, k * BLOCK, column_of(flip_f, flip_cell, first + k * BLOCK))
            for w, (a, flip_f, flip_cell, first) in enumerate(pieces)
            for k in range(a.shape[0] // BLOCK)
        ]

    def moves_of(pieces):
        units = [
            (flip_f ^ 1, flip_cell, first + k * BLOCK)
            for a, flip_f, flip_cell, first in pieces
            for k in range(a.shape[0] // BLOCK)
        ]
        return [(0, u * BLOCK, column_of(*unit)) for u, unit in enumerate(units)]

    half = local_slots // 2

    def place(slot):
        rel = (slot // local_slots) ^ my_f()
        at = slot % local_slots
        index = (rel // 2) * local_slots + ((at // half) ^ (my_cell() % 2)) * half + at % half
        return rel % 2, index

    def multiply(units, pieces, ups, out, received=None, at=(), **other):
        return rows_grad(
            units, [p[0] for p in pieces], *pattern, ups, all_deltas, delta_at, width, out,
            moves_of(at), [] if received is None else [received], **other,
        )

    def row_of(flip, k):
        return lambda: (my_cell() ^ flip) * part + offs[k]

    x0 = over_x(own_rows(0, 0))
    up_sib = over_core(upstream)
    dx = over_x(deltas)
    keep, send, s1, s2, s3 = block_grads(
        place, [2 * local_slots, 2 * local_slots], *pattern, activations, upstream, frozen,
        [(row_of(0, 1), sizes[1]), (row_of(0, 2), sizes[2]), (row_of(3, 2), sizes[2])],
    )

    x0, send, up_sib, s1 = lax.optimization_barrier((x0, send, up_sib, s1))
    y0, z0, x1 = over_y(x0), over_z(x0), over_x(s1)
    gc = over_core(send)

    x1, y0, z0, gc, dx = lax.optimization_barrier((x1, y0, z0, gc, dx))
    dc, dxc = over_core(after(deltas, dx)), over_core(dx)
    gx = over_x(keep[local_slots:] + gc[local_slots:])
    x2 = over_x(after(s2, x1))
    y1, z1 = over_y(x1), over_z(x1)
    yd0 = over_y(z0)
    all_deltas = [deltas, dc, dx, dxc]

    def multiply(units, pieces, ups, out, received=None, at=(), **other):
        return rows_grad(
            units, [p[0] for p in pieces], *pattern, ups, all_deltas, delta_at, width, out,
            moves_of(at), [] if received is None else [received], **other,
        )

    own = [(frozen, 0, None, 0)]
    own_units = units_of(own)
    first_half = len(own_units) // 2
    pieces2 = [(x0, 2, 0, offs[0]), (y0, 2, 2, offs[0]), (z0, 2, 1, offs[0]), (x1, 2, 0, offs[1])]
    n_a = first_half + len(units_of(pieces2))
    out, other_a = multiply(
        own_units[:first_half], own, [upstream, after(up_sib, x1)], None, other_units=n_a
    )

    out, y1, z1, yd0, gx = lax.optimization_barrier((out, y1, z1, yd0, gx))
    owned = keep[:local_slots] + gc[:local_slots] + gx
    gz = over_z(owned[half:])
    yd1 = over_y(z1)
    x3 = over_x(after(s3, z1))
    out, other_a = multiply(
        units_of(pieces2), pieces2, [upstream, after(up_sib, z1)], out,
        other=other_a, other_units=n_a, other_first=first_half * BLOCK,
    )

    out, other_a, x2, yd1, gz = lax.optimization_barrier((out, other_a, x2, yd1, gz))
    y2, z2 = over_y(x2), over_z(x2)
    mine = owned[:half] + gz
    gz2 = over_z(mine, 2)
    oa = over_core(other_a)
    pieces3 = [
        (y1, 2, 2, offs[1]), (z1, 2, 1, offs[1]), (yd0, 2, 3, offs[0]), (yd1, 2, 3, offs[1]),
        (x2, 2, 0, offs[2]),
    ]
    n_3 = len(units_of(pieces3))
    n_b = n_3 + len(own_units) - first_half
    out, other_b = multiply(
        units_of(pieces3), pieces3, [upstream, after(up_sib, x2)], out, other_units=n_b
    )
    out, other_b = multiply(
        own_units[first_half:], own, [upstream, after(up_sib, x2)], out,
        other=other_b, other_units=n_b, other_first=n_3 * BLOCK,
    )

    out, other_b, x3, y2, z2, gz2, oa = lax.optimization_barrier(
        (out, other_b, x3, y2, z2, gz2, oa)
    )
    mine = mine + gz2
    ob = over_core(other_b)
    last = [(x3, 2, 3, offs[2]), (y2, 2, 2, offs[2]), (z2, 2, 1, offs[2])]
    last = last + [(over_core(a), 3, cell, at) for a, _, cell, at in last]
    other_half = over_z(mine)
    own_moves = moves_of(own)

    def moved(m, moves):
        return [(m, u * BLOCK, column) for u, (_, _, column) in enumerate(moves)]

    (out,) = rows_grad(
        units_of(last), [p[0] for p in last], *pattern, [upstream], all_deltas, delta_at, width,
        out,
        moved(0, own_moves[:first_half] + moves_of(pieces2))
        + moved(1, moves_of(pieces3) + own_moves[first_half:]),
        [oa, ob],
    )
    other_half = after(other_half, out)

    normalizer = 1.0 / math.sqrt(upstream.shape[0] * lax.axis_size("fsdp") * n_dp)
    totals = jnp.where(
        lax.axis_index("dp") % 2 == 0,
        jnp.concatenate([mine, other_half], axis=0),
        jnp.concatenate([other_half, mine], axis=0),
    ) * normalizer
    return out, totals


def solution(mesh):
    sizes = dict(mesh.shape)
    cells = sizes["fsdp"] == 4 and sizes["group"] == 2 and sizes["dp"] == 4
    return jax.shard_map(
        relayed if cells else gathered,
        mesh=mesh,
        in_specs=(
            P(("group", "fsdp", "dp"), None),
            P(("group", "fsdp", "dp"), None),
            P("fsdp", None),
            P(("group", "fsdp"), None, None),
            P(),
            P(),
            P(),
        ),
        out_specs=(P(("group", "fsdp", "dp"), None), P(("group", "fsdp"), None, None)),
        check_vma=False,
    )
```

```python
import functools
import math

import jax
import jax.numpy as jnp
from jax import lax
from jax.experimental import pallas as pl
from jax.experimental.pallas import tpu as pltpu
from jax.sharding import PartitionSpec as P

BLOCK = 128
VMEM_BYTES = 48 * 1024 * 1024
GRAD_VMEM_BYTES = 60 * 1024 * 1024
ANY_SPEC = pl.BlockSpec(memory_space=pl.ANY)
HBM_SPEC = pl.BlockSpec(memory_space=pltpu.HBM)
COST = pl.CostEstimate(flops=1024, bytes_accessed=1024, transcendentals=0)
VMEM_SPEC = pl.BlockSpec(memory_space=pltpu.VMEM)


def dot_nt(left, right):
    return lax.dot_general(
        left, right, (((1,), (1,)), ((), ())), preferred_element_type=jnp.float32
    )


def dot_tn(left, right):
    return lax.dot_general(
        left, right, (((0,), (0,)), ((), ())), preferred_element_type=jnp.float32
    )


def after(value, *earlier):
    return lax.optimization_barrier((value, *earlier))[0]


def grad_kernel(place, outs, cuts, rows_hbm, cols_hbm, slots_hbm, act_ref, up_ref, *refs):
    refs = list(refs)
    w_ref = refs.pop(0) if cuts else None
    out_refs, refs = refs[:outs], refs[outs:]
    cut_refs, refs = refs[: len(cuts)], refs[len(cuts) :]
    rows_ref, cols_ref, slots_ref, act_buf, up_buf, sums, *sems = refs
    act_sem, up_sem, i_sem, c_sem, o_sem = sems
    nb = rows_ref.shape[0]
    index_copies = [
        pltpu.make_async_copy(src, dst, i_sem.at[n])
        for n, (src, dst) in enumerate(
            [(rows_hbm, rows_ref), (cols_hbm, cols_ref), (slots_hbm, slots_ref)]
        )
    ]
    for copy in index_copies:
        copy.start()
    up_copy = pltpu.make_async_copy(up_ref, up_buf, up_sem)
    up_copy.start()

    def act_copy(b):
        column = pl.multiple_of(rows_ref[b] * BLOCK, BLOCK)
        return pltpu.make_async_copy(
            act_ref.at[:, pl.ds(column, BLOCK)], act_buf.at[b], act_sem.at[b]
        )

    for copy in index_copies:
        copy.wait()
    for b in range(nb):
        act_copy(b).start()
    cut_copies = [
        pltpu.make_async_copy(
            w_ref.at[pl.ds(pl.multiple_of(first(), BLOCK), ref.shape[0])], ref, c_sem.at[n]
        )
        for n, ((first, _), ref) in enumerate(zip(cuts, cut_refs))
    ]
    for copy in cut_copies:
        copy.start()
    if sums.shape[0] != nb:
        sums[...] = jnp.zeros_like(sums)
    up_copy.wait()
    for b in range(nb):
        act_copy(b).wait()
    for b in range(nb):
        column = pl.multiple_of(cols_ref[b] * BLOCK, BLOCK)
        sums[place(slots_ref[b])] = dot_tn(act_buf[b], up_buf[:, pl.ds(column, BLOCK)])
    first = 0
    out_copies = []
    for n, ref in enumerate(out_refs):
        out_copies.append(
            pltpu.make_async_copy(sums.at[pl.ds(first, ref.shape[0])], ref, o_sem.at[n])
        )
        first += ref.shape[0]
    for copy in out_copies:
        copy.start()
    for copy in out_copies:
        copy.wait()
    for copy in cut_copies:
        copy.wait()


def block_grads(place, shapes, rows, cols, slots, act, up, weight=None, cuts=()):
    nb = rows.shape[0]
    return pl.pallas_call(
        functools.partial(grad_kernel, place, len(shapes), cuts),
        out_shape=[jax.ShapeDtypeStruct((n, BLOCK, BLOCK), jnp.float32) for n in shapes]
        + [jax.ShapeDtypeStruct((n, weight.shape[1]), weight.dtype) for _, n in cuts],
        in_specs=[HBM_SPEC] * (6 if cuts else 5),
        out_specs=[HBM_SPEC] * len(shapes) + [VMEM_SPEC] * len(cuts),
        scratch_shapes=[
            pltpu.SMEM((nb,), jnp.int32),
            pltpu.SMEM((nb,), jnp.int32),
            pltpu.SMEM((nb,), jnp.int32),
            pltpu.VMEM((nb, act.shape[0], BLOCK), act.dtype),
            pltpu.VMEM(up.shape, up.dtype),
            pltpu.VMEM((sum(shapes), BLOCK, BLOCK), jnp.float32),
            pltpu.SemaphoreType.DMA((nb,)),
            pltpu.SemaphoreType.DMA,
            pltpu.SemaphoreType.DMA((3,)),
            pltpu.SemaphoreType.DMA((max(1, len(cuts)),)),
            pltpu.SemaphoreType.DMA((len(shapes),)),
        ],
        compiler_params=pltpu.CompilerParams(vmem_limit_bytes=GRAD_VMEM_BYTES),
        cost_estimate=COST,
        name="block_grads",
    )(rows, cols, slots, act, up, *([weight] if cuts else []))


def rows_kernel(
    units, moves, tile, row_blocks, delta_at, n_up, n_w, n_d, n_m, n_alias, other_first, *refs
):
    refs = list(refs)

    def take(n):
        taken = refs[:n]
        del refs[:n]
        return taken

    rows_hbm, cols_hbm, slots_hbm = take(3)
    up_refs, w_refs, d_refs, m_refs = take(n_up), take(n_w), take(n_d), take(n_m)
    take(n_alias)
    (out_ref,) = take(1)
    other_ref = take(1)[0] if n_up > 1 else None
    rows_ref, cols_ref, slots_ref, up_buf, w_buf, d_buf, acc, o_buf, m_buf = take(9)
    table, head, after_it, i_sem, up_sem, w_sem, d_sem, o_sem, m_sem = take(9)
    nb = rows_ref.shape[0]
    n_units = len(units)
    per = d_buf.shape[0] // n_d
    tokens = up_buf.shape[0] // n_up

    index_copies = [
        pltpu.make_async_copy(src, dst, i_sem.at[n])
        for n, (src, dst) in enumerate(
            [(rows_hbm, rows_ref), (cols_hbm, cols_ref), (slots_hbm, slots_ref)]
        )
    ]
    for copy in index_copies:
        copy.start()
    up_copies = [
        pltpu.make_async_copy(ref, up_buf.at[pl.ds(n * tokens, tokens)], up_sem.at[n])
        for n, ref in enumerate(up_refs)
    ]
    for copy in up_copies:
        copy.start()
    for u, (w, first, _) in enumerate(units):
        pltpu.make_async_copy(
            w_refs[w].at[pl.ds(first, BLOCK)], w_buf.at[pl.ds(u * BLOCK, BLOCK)], w_sem.at[u]
        ).start()
    d_copies = [
        pltpu.make_async_copy(ref, d_buf.at[pl.ds(n * per, per)], d_sem.at[n])
        for n, ref in enumerate(d_refs)
    ]
    for copy in d_copies:
        copy.start()
    m_in = [
        pltpu.make_async_copy(
            m_refs[m].at[:, pl.ds(first, BLOCK)], m_buf.at[n], m_sem.at[0, n]
        )
        for n, (m, first, _) in enumerate(moves)
    ]
    m_out = [
        pltpu.make_async_copy(
            m_buf.at[n],
            out_ref.at[:, pl.ds(pl.multiple_of(column() * BLOCK, BLOCK), BLOCK)],
            m_sem.at[1, n],
        )
        for n, (_, _, column) in enumerate(moves)
    ]
    for copy in m_in:
        copy.start()
    for u, (_, _, column) in enumerate(units):
        table[u] = column()
    for r in range(row_blocks):
        head[r] = -1
    for copy in index_copies:
        copy.wait()
    for b in range(nb):
        r = rows_ref[b]
        after_it[b] = head[r]
        head[r] = b
    for copy in up_copies:
        copy.wait()
    for copy in d_copies:
        copy.wait()

    def out_copies(u):
        column = pl.multiple_of(table[u] * BLOCK, BLOCK)
        copies = [
            pltpu.make_async_copy(
                o_buf.at[u, pl.ds(0, tokens)], out_ref.at[:, pl.ds(column, BLOCK)], o_sem.at[0, u]
            )
        ]
        if other_ref is not None:
            at = other_first + u * BLOCK
            at = at if isinstance(u, int) else pl.multiple_of(at, BLOCK)
            copies.append(
                pltpu.make_async_copy(
                    o_buf.at[u, pl.ds(tokens, tokens)],
                    other_ref.at[:, pl.ds(at, BLOCK)],
                    o_sem.at[1, u],
                )
            )
        return copies

    def step(t, width):
        for h in range(width):
            pltpu.make_async_copy(
                w_refs[0].at[pl.ds(0, BLOCK)],
                w_buf.at[pl.ds((t + h) * BLOCK, BLOCK)],
                w_sem.at[t + h],
            ).wait()
        size = width * BLOCK
        start = t * BLOCK if isinstance(t, int) else pl.multiple_of(t * BLOCK, BLOCK)
        total = dot_nt(up_buf[...], w_buf[pl.ds(start, size)])
        acc[:, :size] = total
        for h in range(width):
            o_buf[t + h] = total[:, h * BLOCK : (h + 1) * BLOCK].astype(o_buf.dtype)
        for h in range(width):
            first_b = head[table[t + h]]

            @pl.when(first_b >= 0)
            def _():
                def add(b):
                    column = pl.multiple_of(cols_ref[b] * BLOCK, BLOCK)
                    delta = d_buf[delta_at(slots_ref[b])]
                    acc[:, h * BLOCK : (h + 1) * BLOCK] += dot_nt(
                        up_buf[:, pl.ds(column, BLOCK)], delta
                    )
                    return after_it[b]

                lax.while_loop(lambda b: b >= 0, add, first_b)
                o_buf[t + h] = acc[:, h * BLOCK : (h + 1) * BLOCK].astype(o_buf.dtype)

        for h in range(width):
            for copy in out_copies(t + h):
                copy.start()

    whole = n_units // tile
    if whole > 1:

        def body(k, carry):
            step(k * tile, tile)
            return carry

        lax.fori_loop(0, whole, body, 0)
    elif whole == 1:
        step(0, tile)
    if n_units % tile:
        step(whole * tile, n_units % tile)

    for copy in m_in:
        copy.wait()
    for copy in m_out:
        copy.start()
    for copy in m_out:
        copy.wait()
    for u in range(n_units):
        for copy in out_copies(u):
            copy.wait()


def rows_grad(
    units, weights, rows, cols, slots, ups, deltas, delta_at, width, out=None, moves=(), moved=(), tile=4,
    other=None, other_units=None, other_first=0, vmem=VMEM_BYTES,
):
    n_units = len(units)
    tile = min(tile, n_units)
    tokens, depth = ups[0].shape
    dtype = ups[0].dtype
    stored = sum(d.shape[0] for d in deltas)
    nb = rows.shape[0]
    operands = [rows, cols, slots, *ups, *weights, *deltas, *moved]
    specs = [HBM_SPEC] * 3 + [ANY_SPEC] * (len(operands) - 3)
    alias = {}
    for n, held in enumerate([out, other]):
        if held is not None:
            alias[len(operands)] = n
            operands.append(held)
            specs.append(HBM_SPEC)
    shapes = [jax.ShapeDtypeStruct((tokens, width), dtype)]
    if len(ups) > 1:
        shapes.append(
            jax.ShapeDtypeStruct((tokens, (other_units or n_units) * BLOCK), dtype)
        )
    return pl.pallas_call(
        functools.partial(
            rows_kernel, units, moves, tile, width // BLOCK, delta_at, len(ups), len(weights),
            len(deltas), len(moved), len(alias), other_first,
        ),
        out_shape=shapes,
        in_specs=specs,
        out_specs=[HBM_SPEC] * len(shapes),
        input_output_aliases=alias,
        scratch_shapes=[
            pltpu.SMEM((nb,), jnp.int32),
            pltpu.SMEM((nb,), jnp.int32),
            pltpu.SMEM((nb,), jnp.int32),
            pltpu.VMEM((len(ups) * tokens, depth), dtype),
            pltpu.VMEM((n_units * BLOCK, depth), dtype),
            pltpu.VMEM((stored, BLOCK, BLOCK), dtype),
            pltpu.VMEM((len(ups) * tokens, tile * BLOCK), jnp.float32),
            pltpu.VMEM((n_units, len(ups) * tokens, BLOCK), dtype),
            pltpu.VMEM((max(1, len(moves)), tokens, BLOCK), dtype),
            pltpu.SMEM((n_units,), jnp.int32),
            pltpu.SMEM((width // BLOCK,), jnp.int32),
            pltpu.SMEM((nb,), jnp.int32),
            pltpu.SemaphoreType.DMA((3,)),
            pltpu.SemaphoreType.DMA((len(ups),)),
            pltpu.SemaphoreType.DMA((n_units,)),
            pltpu.SemaphoreType.DMA((len(deltas),)),
            pltpu.SemaphoreType.DMA((len(ups), n_units)),
            pltpu.SemaphoreType.DMA((2, max(1, len(moves)))),
        ],
        compiler_params=pltpu.CompilerParams(vmem_limit_bytes=vmem),
        cost_estimate=COST,
        name="rows_grad",
    )(*operands)


def gathered(activations, upstream, frozen, deltas, block_rows, block_cols, block_slot):
    local_slots = deltas.shape[0]
    n = lax.axis_size("fsdp")
    width = activations.shape[1]
    pattern = (block_rows, block_cols, block_slot)

    (partial,) = block_grads(
        lambda slot: slot, [n * local_slots], *pattern, activations, upstream
    )
    mine = lax.psum_scatter(partial, "fsdp", scatter_dimension=0, tiled=True)
    totals = lax.psum(mine, "dp")

    all_deltas = lax.all_gather(deltas, "fsdp", axis=0, tiled=True)
    weight = lax.all_gather(frozen, "fsdp", axis=0, tiled=True)
    out = None
    for first in range(0, width, 2048):
        units = [
            (0, first + k * BLOCK, lambda c=first // BLOCK + k: c)
            for k in range(min(2048, width - first) // BLOCK)
        ]
        (out,) = rows_grad(
            units, [weight], *pattern, [upstream], [all_deltas], lambda slot: slot, width, out
        )
    tokens = upstream.shape[0] * n * lax.axis_size("dp")
    return out, totals * (1.0 / math.sqrt(tokens))


def relayed(activations, upstream, frozen, deltas, block_rows, block_cols, block_slot):
    local_slots = deltas.shape[0]
    quarter = frozen.shape[0]
    width = activations.shape[1]
    n_dp = lax.axis_size("dp")
    pattern = (block_rows, block_cols, block_slot)

    def my_f():
        return lax.axis_index("fsdp")

    def my_cell():
        return 2 * lax.axis_index("group") + lax.axis_index("dp") % 2

    def over_core(a):
        return lax.ppermute(a, "fsdp", [(k, k ^ 1) for k in range(4)])

    def over_x(a):
        return lax.ppermute(a, "fsdp", [(k, k ^ 2) for k in range(4)])

    def over_y(a):
        return lax.ppermute(a, "group", [(k, k ^ 1) for k in range(2)])

    def over_z(a, step=1):
        return lax.ppermute(a, "dp", [(k, k ^ step) for k in range(n_dp)])

    part = quarter // 4
    sizes = (part // 4, part // 4, part // 2)
    offs = (0, sizes[0], sizes[0] + sizes[1])

    def row_of(flip, k):
        return lambda: (my_cell() ^ flip) * part + offs[k]

    def delta_at(slot):
        return ((slot // local_slots) ^ my_f()) * local_slots + slot % local_slots

    def column_of(flip_f, flip_cell, at):
        def column():
            base = (my_f() ^ flip_f) * (quarter // BLOCK) + at // BLOCK
            if flip_cell is not None:
                base = base + (my_cell() ^ flip_cell) * (part // BLOCK)
            return base

        return column

    def units_of(pieces):
        return [
            (w, k * BLOCK, column_of(flip_f, flip_cell, first + k * BLOCK))
            for w, (a, flip_f, flip_cell, first) in enumerate(pieces)
            for k in range(a.shape[0] // BLOCK)
        ]

    def moves_of(pieces):
        units = [
            (flip_f ^ 1, flip_cell, first + k * BLOCK)
            for a, flip_f, flip_cell, first in pieces
            for k in range(a.shape[0] // BLOCK)
        ]
        return [(0, u * BLOCK, column_of(*unit)) for u, unit in enumerate(units)]

    half = local_slots // 2

    def place(slot):
        rel = (slot // local_slots) ^ my_f()
        at = slot % local_slots
        index = ((at // half) ^ (lax.axis_index("dp") % 2)) * half + at % half
        return ((rel % 2) * 2 + rel // 2) * local_slots + index

    x0 = over_x(lax.dynamic_slice_in_dim(frozen, my_cell() * part, sizes[0], 0))
    up_sib = over_core(upstream)
    dc = over_core(deltas)
    dx = over_x(deltas)
    keep, send, s1, s2, s3 = block_grads(
        place, [2 * local_slots, 2 * local_slots], *pattern, activations, upstream, frozen,
        [(row_of(0, 1), sizes[1]), (row_of(0, 2), sizes[2]), (row_of(3, 1), sizes[1] + sizes[2])],
    )

    x0, send, up_sib, s1, s2, dc, dx = lax.optimization_barrier(
        (x0, send, up_sib, s1, s2, dc, dx)
    )
    y0, z0, x1 = over_y(x0), over_z(x0), over_x(s1)
    gc = over_core(send)
    gx = over_x(keep[local_slots:] + gc[local_slots:])

    dxc = over_core(dx)
    all_deltas = [deltas, dc, dx, dxc]

    def multiply(pieces, ups, out, at=(), moved=(), units=None, **other):
        moves = [
            (m, first, column)
            for m, there in enumerate(at)
            for _, first, column in moves_of(there)
        ]
        return rows_grad(
            units or units_of(pieces), [p[0] for p in pieces], *pattern, ups, all_deltas, delta_at,
            width, out, moves, moved, **other,
        )

    pieces1 = [(frozen, 0, None, 0)]
    units1 = units_of(pieces1)
    first_half = len(units1) // 2
    out, other1 = multiply(
        pieces1, [upstream, after(up_sib, x0)], None, units=units1[:first_half],
        other_units=len(units1),
    )

    x1, y0, z0, gx, s2, out, other1 = lax.optimization_barrier(
        (x1, y0, z0, gx, s2, out, other1)
    )
    x2 = over_x(s2)
    y1, z1, yd = over_y(x1), over_z(x1), over_y(z0)
    owned = keep[:local_slots] + gc[:local_slots] + gx
    gz = over_z(owned[half:])
    out, other1 = multiply(
        pieces1, [upstream, after(up_sib, x1)], out, units=units1[first_half:],
        other=other1, other_units=len(units1), other_first=first_half * BLOCK,
    )

    out, other1, gz, x2, y1, z1, yd = lax.optimization_barrier(
        (out, other1, gz, x2, y1, z1, yd)
    )
    y2, z2 = over_y(x2), over_z(x2)
    x3 = over_x(after(s3, x2))
    mine = owned[:half] + gz
    gz2 = over_z(mine, 2)
    o1 = over_core(other1)
    pieces2 = [
        (x0, 2, 0, offs[0]), (y0, 2, 2, offs[0]), (z0, 2, 1, offs[0]), (x1, 2, 0, offs[1]),
        (y1, 2, 2, offs[1]), (z1, 2, 1, offs[1]), (yd, 2, 3, offs[0]), (x2, 2, 0, offs[2]),
    ]
    out, other2 = multiply(pieces2, [upstream, after(up_sib, x2)], out, [pieces1], [o1])

    out, other2, x3, y2, z2, gz2 = lax.optimization_barrier((out, other2, x3, y2, z2, gz2))
    mine = mine + gz2
    other_half = over_z(mine)
    o2 = over_core(other2)
    last = [(x3, 2, 3, offs[1]), (y2, 2, 2, offs[2]), (z2, 2, 1, offs[2])]
    last = last + [(over_core(a), 3, cell, at) for a, _, cell, at in last]
    (out,) = multiply(last, [upstream], out, [pieces2], [o2])
    other_half = after(other_half, out)
    normalizer = 1.0 / math.sqrt(upstream.shape[0] * lax.axis_size("fsdp") * n_dp)
    totals = jnp.where(
        lax.axis_index("dp") % 2 == 0,
        jnp.concatenate([mine, other_half], axis=0),
        jnp.concatenate([other_half, mine], axis=0),
    ) * normalizer
    return out, totals


def solution(mesh):
    sizes = dict(mesh.shape)
    cells = sizes["fsdp"] == 4 and sizes["group"] == 2 and sizes["dp"] == 4
    return jax.shard_map(
        relayed if cells else gathered,
        mesh=mesh,
        in_specs=(
            P(("group", "fsdp", "dp"), None),
            P(("group", "fsdp", "dp"), None),
            P("fsdp", None),
            P(("group", "fsdp"), None, None),
            P(),
            P(),
            P(),
        ),
        out_specs=(P(("group", "fsdp", "dp"), None), P(("group", "fsdp"), None, None)),
        check_vma=False,
    )
```

```python
import functools
import math

import jax
import jax.numpy as jnp
from jax import lax
from jax.experimental import pallas as pl
from jax.experimental.pallas import tpu as pltpu
from jax.sharding import PartitionSpec as P

BLOCK = 128
VMEM_BYTES = 48 * 1024 * 1024
GRAD_VMEM_BYTES = 60 * 1024 * 1024
ANY_SPEC = pl.BlockSpec(memory_space=pl.ANY)
HBM_SPEC = pl.BlockSpec(memory_space=pltpu.HBM)
COST = pl.CostEstimate(flops=1024, bytes_accessed=1024, transcendentals=0)
VMEM_SPEC = pl.BlockSpec(memory_space=pltpu.VMEM)


def dot_nt(left, right):
    return lax.dot_general(
        left, right, (((1,), (1,)), ((), ())), preferred_element_type=jnp.float32
    )


def dot_tn(left, right):
    return lax.dot_general(
        left, right, (((0,), (0,)), ((), ())), preferred_element_type=jnp.float32
    )


def after(value, *earlier):
    return lax.optimization_barrier((value, *earlier))[0]


def grad_kernel(place, outs, cuts, rows_hbm, cols_hbm, slots_hbm, act_ref, up_ref, *refs):
    refs = list(refs)
    w_ref = refs.pop(0) if cuts else None
    out_refs, refs = refs[:outs], refs[outs:]
    cut_refs, refs = refs[: len(cuts)], refs[len(cuts) :]
    rows_ref, cols_ref, slots_ref, act_buf, up_buf, sums, *sems = refs
    act_sem, up_sem, i_sem, c_sem, o_sem = sems
    nb = rows_ref.shape[0]
    index_copies = [
        pltpu.make_async_copy(src, dst, i_sem.at[n])
        for n, (src, dst) in enumerate(
            [(rows_hbm, rows_ref), (cols_hbm, cols_ref), (slots_hbm, slots_ref)]
        )
    ]
    for copy in index_copies:
        copy.start()
    up_copy = pltpu.make_async_copy(up_ref, up_buf, up_sem)
    up_copy.start()

    def act_copy(b):
        column = pl.multiple_of(rows_ref[b] * BLOCK, BLOCK)
        return pltpu.make_async_copy(
            act_ref.at[:, pl.ds(column, BLOCK)], act_buf.at[b], act_sem.at[b]
        )

    for copy in index_copies:
        copy.wait()
    for b in range(nb):
        act_copy(b).start()
    cut_copies = [
        pltpu.make_async_copy(
            w_ref.at[pl.ds(pl.multiple_of(first(), BLOCK), ref.shape[0])], ref, c_sem.at[n]
        )
        for n, ((first, _), ref) in enumerate(zip(cuts, cut_refs))
    ]
    for copy in cut_copies:
        copy.start()
    if sums.shape[0] != nb:
        sums[...] = jnp.zeros_like(sums)
    up_copy.wait()
    for b in range(nb):
        act_copy(b).wait()
    for b in range(nb):
        column = pl.multiple_of(cols_ref[b] * BLOCK, BLOCK)
        sums[place(slots_ref[b])] = dot_tn(act_buf[b], up_buf[:, pl.ds(column, BLOCK)])
    first = 0
    out_copies = []
    for n, ref in enumerate(out_refs):
        out_copies.append(
            pltpu.make_async_copy(sums.at[pl.ds(first, ref.shape[0])], ref, o_sem.at[n])
        )
        first += ref.shape[0]
    for copy in out_copies:
        copy.start()
    for copy in out_copies:
        copy.wait()
    for copy in cut_copies:
        copy.wait()


def block_grads(place, shapes, rows, cols, slots, act, up, weight=None, cuts=()):
    nb = rows.shape[0]
    return pl.pallas_call(
        functools.partial(grad_kernel, place, len(shapes), cuts),
        out_shape=[jax.ShapeDtypeStruct((n, BLOCK, BLOCK), jnp.float32) for n in shapes]
        + [jax.ShapeDtypeStruct((n, weight.shape[1]), weight.dtype) for _, n in cuts],
        in_specs=[HBM_SPEC] * (6 if cuts else 5),
        out_specs=[HBM_SPEC] * len(shapes) + [VMEM_SPEC] * len(cuts),
        scratch_shapes=[
            pltpu.SMEM((nb,), jnp.int32),
            pltpu.SMEM((nb,), jnp.int32),
            pltpu.SMEM((nb,), jnp.int32),
            pltpu.VMEM((nb, act.shape[0], BLOCK), act.dtype),
            pltpu.VMEM(up.shape, up.dtype),
            pltpu.VMEM((sum(shapes), BLOCK, BLOCK), jnp.float32),
            pltpu.SemaphoreType.DMA((nb,)),
            pltpu.SemaphoreType.DMA,
            pltpu.SemaphoreType.DMA((3,)),
            pltpu.SemaphoreType.DMA((max(1, len(cuts)),)),
            pltpu.SemaphoreType.DMA((len(shapes),)),
        ],
        compiler_params=pltpu.CompilerParams(vmem_limit_bytes=GRAD_VMEM_BYTES),
        cost_estimate=COST,
        name="block_grads",
    )(rows, cols, slots, act, up, *([weight] if cuts else []))


def rows_kernel(
    units, moves, tile, row_blocks, delta_at, n_up, n_w, n_d, n_m, n_alias, other_first, *refs
):
    refs = list(refs)

    def take(n):
        taken = refs[:n]
        del refs[:n]
        return taken

    rows_hbm, cols_hbm, slots_hbm = take(3)
    up_refs, w_refs, d_refs, m_refs = take(n_up), take(n_w), take(n_d), take(n_m)
    take(n_alias)
    (out_ref,) = take(1)
    other_ref = take(1)[0] if n_up > 1 else None
    rows_ref, cols_ref, slots_ref, up_buf, w_buf, d_buf, acc, o_buf, m_buf = take(9)
    table, head, after_it, i_sem, up_sem, w_sem, d_sem, o_sem, m_sem = take(9)
    nb = rows_ref.shape[0]
    n_units = len(units)
    per = d_buf.shape[0] // n_d
    tokens = up_buf.shape[0] // n_up

    index_copies = [
        pltpu.make_async_copy(src, dst, i_sem.at[n])
        for n, (src, dst) in enumerate(
            [(rows_hbm, rows_ref), (cols_hbm, cols_ref), (slots_hbm, slots_ref)]
        )
    ]
    for copy in index_copies:
        copy.start()
    up_copies = [
        pltpu.make_async_copy(ref, up_buf.at[pl.ds(n * tokens, tokens)], up_sem.at[n])
        for n, ref in enumerate(up_refs)
    ]
    for copy in up_copies:
        copy.start()
    for u, (w, first, _) in enumerate(units):
        pltpu.make_async_copy(
            w_refs[w].at[pl.ds(first, BLOCK)], w_buf.at[pl.ds(u * BLOCK, BLOCK)], w_sem.at[u]
        ).start()
    d_copies = [
        pltpu.make_async_copy(ref, d_buf.at[pl.ds(n * per, per)], d_sem.at[n])
        for n, ref in enumerate(d_refs)
    ]
    for copy in d_copies:
        copy.start()
    m_in = [
        pltpu.make_async_copy(
            m_refs[m].at[:, pl.ds(first, BLOCK)], m_buf.at[n], m_sem.at[0, n]
        )
        for n, (m, first, _) in enumerate(moves)
    ]
    m_out = [
        pltpu.make_async_copy(
            m_buf.at[n],
            out_ref.at[:, pl.ds(pl.multiple_of(column() * BLOCK, BLOCK), BLOCK)],
            m_sem.at[1, n],
        )
        for n, (_, _, column) in enumerate(moves)
    ]
    for copy in m_in:
        copy.start()
    for u, (_, _, column) in enumerate(units):
        table[u] = column()
    for r in range(row_blocks):
        head[r] = -1
    for copy in index_copies:
        copy.wait()
    for b in range(nb):
        r = rows_ref[b]
        after_it[b] = head[r]
        head[r] = b
    for copy in up_copies:
        copy.wait()
    for copy in d_copies:
        copy.wait()

    def out_copies(u):
        column = pl.multiple_of(table[u] * BLOCK, BLOCK)
        copies = [
            pltpu.make_async_copy(
                o_buf.at[u, pl.ds(0, tokens)], out_ref.at[:, pl.ds(column, BLOCK)], o_sem.at[0, u]
            )
        ]
        if other_ref is not None:
            at = other_first + u * BLOCK
            at = at if isinstance(u, int) else pl.multiple_of(at, BLOCK)
            copies.append(
                pltpu.make_async_copy(
                    o_buf.at[u, pl.ds(tokens, tokens)],
                    other_ref.at[:, pl.ds(at, BLOCK)],
                    o_sem.at[1, u],
                )
            )
        return copies

    def step(t, width):
        for h in range(width):
            pltpu.make_async_copy(
                w_refs[0].at[pl.ds(0, BLOCK)],
                w_buf.at[pl.ds((t + h) * BLOCK, BLOCK)],
                w_sem.at[t + h],
            ).wait()
        size = width * BLOCK
        start = t * BLOCK if isinstance(t, int) else pl.multiple_of(t * BLOCK, BLOCK)
        total = dot_nt(up_buf[...], w_buf[pl.ds(start, size)])
        acc[:, :size] = total
        for h in range(width):
            o_buf[t + h] = total[:, h * BLOCK : (h + 1) * BLOCK].astype(o_buf.dtype)
        for h in range(width):
            first_b = head[table[t + h]]

            @pl.when(first_b >= 0)
            def _():
                def add(b):
                    column = pl.multiple_of(cols_ref[b] * BLOCK, BLOCK)
                    delta = d_buf[delta_at(slots_ref[b])]
                    acc[:, h * BLOCK : (h + 1) * BLOCK] += dot_nt(
                        up_buf[:, pl.ds(column, BLOCK)], delta
                    )
                    return after_it[b]

                lax.while_loop(lambda b: b >= 0, add, first_b)
                o_buf[t + h] = acc[:, h * BLOCK : (h + 1) * BLOCK].astype(o_buf.dtype)

        for h in range(width):
            for copy in out_copies(t + h):
                copy.start()

    whole = n_units // tile
    if whole > 1:

        def body(k, carry):
            step(k * tile, tile)
            return carry

        lax.fori_loop(0, whole, body, 0)
    elif whole == 1:
        step(0, tile)
    if n_units % tile:
        step(whole * tile, n_units % tile)

    for copy in m_in:
        copy.wait()
    for copy in m_out:
        copy.start()
    for copy in m_out:
        copy.wait()
    for u in range(n_units):
        for copy in out_copies(u):
            copy.wait()


def rows_grad(
    units, weights, rows, cols, slots, ups, deltas, delta_at, width, out=None, moves=(), moved=(), tile=4,
    other=None, other_units=None, other_first=0, vmem=VMEM_BYTES,
):
    n_units = len(units)
    tile = min(tile, n_units)
    tokens, depth = ups[0].shape
    dtype = ups[0].dtype
    stored = sum(d.shape[0] for d in deltas)
    nb = rows.shape[0]
    operands = [rows, cols, slots, *ups, *weights, *deltas, *moved]
    specs = [HBM_SPEC] * 3 + [ANY_SPEC] * (len(operands) - 3)
    alias = {}
    for n, held in enumerate([out, other]):
        if held is not None:
            alias[len(operands)] = n
            operands.append(held)
            specs.append(HBM_SPEC)
    shapes = [jax.ShapeDtypeStruct((tokens, width), dtype)]
    if len(ups) > 1:
        shapes.append(
            jax.ShapeDtypeStruct((tokens, (other_units or n_units) * BLOCK), dtype)
        )
    return pl.pallas_call(
        functools.partial(
            rows_kernel, units, moves, tile, width // BLOCK, delta_at, len(ups), len(weights),
            len(deltas), len(moved), len(alias), other_first,
        ),
        out_shape=shapes,
        in_specs=specs,
        out_specs=[HBM_SPEC] * len(shapes),
        input_output_aliases=alias,
        scratch_shapes=[
            pltpu.SMEM((nb,), jnp.int32),
            pltpu.SMEM((nb,), jnp.int32),
            pltpu.SMEM((nb,), jnp.int32),
            pltpu.VMEM((len(ups) * tokens, depth), dtype),
            pltpu.VMEM((n_units * BLOCK, depth), dtype),
            pltpu.VMEM((stored, BLOCK, BLOCK), dtype),
            pltpu.VMEM((len(ups) * tokens, tile * BLOCK), jnp.float32),
            pltpu.VMEM((n_units, len(ups) * tokens, BLOCK), dtype),
            pltpu.VMEM((max(1, len(moves)), tokens, BLOCK), dtype),
            pltpu.SMEM((n_units,), jnp.int32),
            pltpu.SMEM((width // BLOCK,), jnp.int32),
            pltpu.SMEM((nb,), jnp.int32),
            pltpu.SemaphoreType.DMA((3,)),
            pltpu.SemaphoreType.DMA((len(ups),)),
            pltpu.SemaphoreType.DMA((n_units,)),
            pltpu.SemaphoreType.DMA((len(deltas),)),
            pltpu.SemaphoreType.DMA((len(ups), n_units)),
            pltpu.SemaphoreType.DMA((2, max(1, len(moves)))),
        ],
        compiler_params=pltpu.CompilerParams(vmem_limit_bytes=vmem),
        cost_estimate=COST,
        name="rows_grad",
    )(*operands)


def gathered(activations, upstream, frozen, deltas, block_rows, block_cols, block_slot):
    local_slots = deltas.shape[0]
    n = lax.axis_size("fsdp")
    width = activations.shape[1]
    pattern = (block_rows, block_cols, block_slot)

    (partial,) = block_grads(
        lambda slot: slot, [n * local_slots], *pattern, activations, upstream
    )
    mine = lax.psum_scatter(partial, "fsdp", scatter_dimension=0, tiled=True)
    totals = lax.psum(mine, "dp")

    all_deltas = lax.all_gather(deltas, "fsdp", axis=0, tiled=True)
    weight = lax.all_gather(frozen, "fsdp", axis=0, tiled=True)
    out = None
    for first in range(0, width, 2048):
        units = [
            (0, first + k * BLOCK, lambda c=first // BLOCK + k: c)
            for k in range(min(2048, width - first) // BLOCK)
        ]
        (out,) = rows_grad(
            units, [weight], *pattern, [upstream], [all_deltas], lambda slot: slot, width, out
        )
    tokens = upstream.shape[0] * n * lax.axis_size("dp")
    return out, totals * (1.0 / math.sqrt(tokens))


def relayed(activations, upstream, frozen, deltas, block_rows, block_cols, block_slot):
    local_slots = deltas.shape[0]
    quarter = frozen.shape[0]
    width = activations.shape[1]
    n_dp = lax.axis_size("dp")
    pattern = (block_rows, block_cols, block_slot)

    def my_f():
        return lax.axis_index("fsdp")

    def my_cell():
        return 2 * lax.axis_index("group") + lax.axis_index("dp") % 2

    def over_core(a):
        return lax.ppermute(a, "fsdp", [(k, k ^ 1) for k in range(4)])

    def over_x(a):
        return lax.ppermute(a, "fsdp", [(k, k ^ 2) for k in range(4)])

    def over_y(a):
        return lax.ppermute(a, "group", [(k, k ^ 1) for k in range(2)])

    def over_z(a, step=1):
        return lax.ppermute(a, "dp", [(k, k ^ step) for k in range(n_dp)])

    part = quarter // 4
    sizes = (part // 4, part // 4, part // 2)
    offs = (0, sizes[0], sizes[0] + sizes[1])

    def row_of(flip, k):
        return lambda: (my_cell() ^ flip) * part + offs[k]

    def delta_at(slot):
        return ((slot // local_slots) ^ my_f()) * local_slots + slot % local_slots

    def column_of(flip_f, flip_cell, at):
        def column():
            base = (my_f() ^ flip_f) * (quarter // BLOCK) + at // BLOCK
            if flip_cell is not None:
                base = base + (my_cell() ^ flip_cell) * (part // BLOCK)
            return base

        return column

    def units_of(pieces):
        return [
            (w, k * BLOCK, column_of(flip_f, flip_cell, first + k * BLOCK))
            for w, (a, flip_f, flip_cell, first) in enumerate(pieces)
            for k in range(a.shape[0] // BLOCK)
        ]

    def moves_of(pieces):
        units = [
            (flip_f ^ 1, flip_cell, first + k * BLOCK)
            for a, flip_f, flip_cell, first in pieces
            for k in range(a.shape[0] // BLOCK)
        ]
        return [(0, u * BLOCK, column_of(*unit)) for u, unit in enumerate(units)]

    half = local_slots // 2

    def place(slot):
        rel = (slot // local_slots) ^ my_f()
        at = slot % local_slots
        index = ((at // half) ^ (lax.axis_index("dp") % 2)) * half + at % half
        return ((rel % 2) * 2 + rel // 2) * local_slots + index

    x0 = over_x(lax.dynamic_slice_in_dim(frozen, my_cell() * part, sizes[0], 0))
    up_sib = over_core(upstream)
    dc = over_core(deltas)
    dx = over_x(deltas)
    keep, send, s1, s2, s3 = block_grads(
        place, [2 * local_slots, 2 * local_slots], *pattern, activations, upstream, frozen,
        [(row_of(0, 1), sizes[1]), (row_of(0, 2), sizes[2]), (row_of(3, 1), sizes[1] + sizes[2])],
    )

    x0, send, up_sib, s1, s2, dc, dx = lax.optimization_barrier(
        (x0, send, up_sib, s1, s2, dc, dx)
    )
    y0, z0, x1 = over_y(x0), over_z(x0), over_x(s1)
    gc = over_core(send)
    gx = over_x(keep[local_slots:] + gc[local_slots:])

    dxc = over_core(dx)
    all_deltas = [deltas, dc, dx, dxc]

    def multiply(pieces, ups, out, at=(), moved=(), units=None, **other):
        moves = [
            (m, first, column)
            for m, there in enumerate(at)
            for _, first, column in moves_of(there)
        ]
        return rows_grad(
            units or units_of(pieces), [p[0] for p in pieces], *pattern, ups, all_deltas, delta_at,
            width, out, moves, moved, **other,
        )

    pieces1 = [(frozen, 0, None, 0)]
    units1 = units_of(pieces1)
    first_half = len(units1) // 2
    out, other1 = multiply(
        pieces1, [upstream, after(up_sib, x0)], None, units=units1[:first_half],
        other_units=len(units1),
    )

    gx, s2, out, other1, x1 = lax.optimization_barrier((gx, s2, out, other1, x1))
    y0, z0 = lax.optimization_barrier((y0, z0))
    x2 = over_x(s2)
    y1, z1, yd = over_y(x1), over_z(x1), over_y(z0)
    owned = keep[:local_slots] + gc[:local_slots] + gx
    gz = over_z(owned[half:])
    out, other1 = multiply(
        pieces1, [upstream, after(up_sib, x1)], out, units=units1[first_half:],
        other=other1, other_units=len(units1), other_first=first_half * BLOCK,
    )

    out, other1, gz, x2, y1, z1, yd = lax.optimization_barrier(
        (out, other1, gz, x2, y1, z1, yd)
    )
    y2, z2 = over_y(x2), over_z(x2)
    x3 = over_x(after(s3, x2))
    mine = owned[:half] + gz
    gz2 = over_z(mine, 2)
    o1 = over_core(other1)
    pieces2 = [
        (x0, 2, 0, offs[0]), (y0, 2, 2, offs[0]), (z0, 2, 1, offs[0]), (x1, 2, 0, offs[1]),
        (y1, 2, 2, offs[1]), (z1, 2, 1, offs[1]), (yd, 2, 3, offs[0]), (x2, 2, 0, offs[2]),
    ]
    out, other2 = multiply(pieces2, [upstream, after(up_sib, x2)], out, [pieces1], [o1])

    out, other2, x3, y2, z2, gz2 = lax.optimization_barrier((out, other2, x3, y2, z2, gz2))
    mine = mine + gz2
    other_half = over_z(mine)
    o2 = over_core(other2)
    last = [(x3, 2, 3, offs[1]), (y2, 2, 2, offs[2]), (z2, 2, 1, offs[2])]
    last = last + [(over_core(a), 3, cell, at) for a, _, cell, at in last]
    (out,) = multiply(last, [upstream], out, [pieces2], [o2])
    other_half = after(other_half, out)
    normalizer = 1.0 / math.sqrt(upstream.shape[0] * lax.axis_size("fsdp") * n_dp)
    totals = jnp.where(
        lax.axis_index("dp") % 2 == 0,
        jnp.concatenate([mine, other_half], axis=0),
        jnp.concatenate([other_half, mine], axis=0),
    ) * normalizer
    return out, totals


def solution(mesh):
    sizes = dict(mesh.shape)
    cells = sizes["fsdp"] == 4 and sizes["group"] == 2 and sizes["dp"] == 4
    return jax.shard_map(
        relayed if cells else gathered,
        mesh=mesh,
        in_specs=(
            P(("group", "fsdp", "dp"), None),
            P(("group", "fsdp", "dp"), None),
            P("fsdp", None),
            P(("group", "fsdp"), None, None),
            P(),
            P(),
            P(),
        ),
        out_specs=(P(("group", "fsdp", "dp"), None), P(("group", "fsdp"), None, None)),
        check_vma=False,
    )
```

```python
import functools
import math

import jax
import jax.numpy as jnp
from jax import lax
from jax.experimental import pallas as pl
from jax.experimental.pallas import tpu as pltpu
from jax.sharding import PartitionSpec as P

BLOCK = 128
VMEM_BYTES = 48 * 1024 * 1024
GRAD_VMEM_BYTES = 60 * 1024 * 1024
ANY_SPEC = pl.BlockSpec(memory_space=pl.ANY)
HBM_SPEC = pl.BlockSpec(memory_space=pltpu.HBM)
COST = pl.CostEstimate(flops=1024, bytes_accessed=1024, transcendentals=0)
VMEM_SPEC = pl.BlockSpec(memory_space=pltpu.VMEM)


def dot_nt(left, right):
    return lax.dot_general(
        left, right, (((1,), (1,)), ((), ())), preferred_element_type=jnp.float32
    )


def dot_tn(left, right):
    return lax.dot_general(
        left, right, (((0,), (0,)), ((), ())), preferred_element_type=jnp.float32
    )


def after(value, *earlier):
    return lax.optimization_barrier((value, *earlier))[0]


def grad_kernel(place, outs, cuts, rows_hbm, cols_hbm, slots_hbm, act_ref, up_ref, *refs):
    refs = list(refs)
    w_ref = refs.pop(0) if cuts else None
    out_refs, refs = refs[:outs], refs[outs:]
    cut_refs, refs = refs[: len(cuts)], refs[len(cuts) :]
    rows_ref, cols_ref, slots_ref, act_buf, up_buf, sums, *sems = refs
    act_sem, up_sem, i_sem, c_sem, o_sem = sems
    nb = rows_ref.shape[0]
    index_copies = [
        pltpu.make_async_copy(src, dst, i_sem.at[n])
        for n, (src, dst) in enumerate(
            [(rows_hbm, rows_ref), (cols_hbm, cols_ref), (slots_hbm, slots_ref)]
        )
    ]
    for copy in index_copies:
        copy.start()
    up_copy = pltpu.make_async_copy(up_ref, up_buf, up_sem)
    up_copy.start()

    def act_copy(b):
        column = pl.multiple_of(rows_ref[b] * BLOCK, BLOCK)
        return pltpu.make_async_copy(
            act_ref.at[:, pl.ds(column, BLOCK)], act_buf.at[b], act_sem.at[b]
        )

    for copy in index_copies:
        copy.wait()
    for b in range(nb):
        act_copy(b).start()
    cut_copies = [
        pltpu.make_async_copy(
            w_ref.at[pl.ds(pl.multiple_of(first(), BLOCK), ref.shape[0])], ref, c_sem.at[n]
        )
        for n, ((first, _), ref) in enumerate(zip(cuts, cut_refs))
    ]
    for copy in cut_copies:
        copy.start()
    if sums.shape[0] != nb:
        sums[...] = jnp.zeros_like(sums)
    up_copy.wait()
    for b in range(nb):
        act_copy(b).wait()
    for b in range(nb):
        column = pl.multiple_of(cols_ref[b] * BLOCK, BLOCK)
        sums[place(slots_ref[b])] = dot_tn(act_buf[b], up_buf[:, pl.ds(column, BLOCK)])
    first = 0
    out_copies = []
    for n, ref in enumerate(out_refs):
        out_copies.append(
            pltpu.make_async_copy(sums.at[pl.ds(first, ref.shape[0])], ref, o_sem.at[n])
        )
        first += ref.shape[0]
    for copy in out_copies:
        copy.start()
    for copy in out_copies:
        copy.wait()
    for copy in cut_copies:
        copy.wait()


def block_grads(place, shapes, rows, cols, slots, act, up, weight=None, cuts=()):
    nb = rows.shape[0]
    return pl.pallas_call(
        functools.partial(grad_kernel, place, len(shapes), cuts),
        out_shape=[jax.ShapeDtypeStruct((n, BLOCK, BLOCK), jnp.float32) for n in shapes]
        + [jax.ShapeDtypeStruct((n, weight.shape[1]), weight.dtype) for _, n in cuts],
        in_specs=[HBM_SPEC] * (6 if cuts else 5),
        out_specs=[HBM_SPEC] * len(shapes) + [VMEM_SPEC] * len(cuts),
        scratch_shapes=[
            pltpu.SMEM((nb,), jnp.int32),
            pltpu.SMEM((nb,), jnp.int32),
            pltpu.SMEM((nb,), jnp.int32),
            pltpu.VMEM((nb, act.shape[0], BLOCK), act.dtype),
            pltpu.VMEM(up.shape, up.dtype),
            pltpu.VMEM((sum(shapes), BLOCK, BLOCK), jnp.float32),
            pltpu.SemaphoreType.DMA((nb,)),
            pltpu.SemaphoreType.DMA,
            pltpu.SemaphoreType.DMA((3,)),
            pltpu.SemaphoreType.DMA((max(1, len(cuts)),)),
            pltpu.SemaphoreType.DMA((len(shapes),)),
        ],
        compiler_params=pltpu.CompilerParams(vmem_limit_bytes=GRAD_VMEM_BYTES),
        cost_estimate=COST,
        name="block_grads",
    )(rows, cols, slots, act, up, *([weight] if cuts else []))


def rows_kernel(
    units, moves, tile, row_blocks, delta_at, n_up, n_w, n_d, n_m, n_alias, other_first, *refs
):
    refs = list(refs)

    def take(n):
        taken = refs[:n]
        del refs[:n]
        return taken

    rows_hbm, cols_hbm, slots_hbm = take(3)
    up_refs, w_refs, d_refs, m_refs = take(n_up), take(n_w), take(n_d), take(n_m)
    take(n_alias)
    (out_ref,) = take(1)
    other_ref = take(1)[0] if n_up > 1 else None
    rows_ref, cols_ref, slots_ref, up_buf, w_buf, d_buf, acc, o_buf, m_buf = take(9)
    table, head, after_it, i_sem, up_sem, w_sem, d_sem, o_sem, m_sem = take(9)
    nb = rows_ref.shape[0]
    n_units = len(units)
    per = d_buf.shape[0] // n_d
    tokens = up_buf.shape[0] // n_up

    index_copies = [
        pltpu.make_async_copy(src, dst, i_sem.at[n])
        for n, (src, dst) in enumerate(
            [(rows_hbm, rows_ref), (cols_hbm, cols_ref), (slots_hbm, slots_ref)]
        )
    ]
    for copy in index_copies:
        copy.start()
    up_copies = [
        pltpu.make_async_copy(ref, up_buf.at[pl.ds(n * tokens, tokens)], up_sem.at[n])
        for n, ref in enumerate(up_refs)
    ]
    for copy in up_copies:
        copy.start()
    for u, (w, first, _) in enumerate(units):
        pltpu.make_async_copy(
            w_refs[w].at[pl.ds(first, BLOCK)], w_buf.at[pl.ds(u * BLOCK, BLOCK)], w_sem.at[u]
        ).start()
    d_copies = [
        pltpu.make_async_copy(ref, d_buf.at[pl.ds(n * per, per)], d_sem.at[n])
        for n, ref in enumerate(d_refs)
    ]
    for copy in d_copies:
        copy.start()
    m_in = [
        pltpu.make_async_copy(
            m_refs[m].at[:, pl.ds(first, BLOCK)], m_buf.at[n], m_sem.at[0, n]
        )
        for n, (m, first, _) in enumerate(moves)
    ]
    m_out = [
        pltpu.make_async_copy(
            m_buf.at[n],
            out_ref.at[:, pl.ds(pl.multiple_of(column() * BLOCK, BLOCK), BLOCK)],
            m_sem.at[1, n],
        )
        for n, (_, _, column) in enumerate(moves)
    ]
    for copy in m_in:
        copy.start()
    for u, (_, _, column) in enumerate(units):
        table[u] = column()
    for r in range(row_blocks):
        head[r] = -1
    for copy in index_copies:
        copy.wait()
    for b in range(nb):
        r = rows_ref[b]
        after_it[b] = head[r]
        head[r] = b
    for copy in up_copies:
        copy.wait()
    for copy in d_copies:
        copy.wait()

    def out_copies(u):
        column = pl.multiple_of(table[u] * BLOCK, BLOCK)
        copies = [
            pltpu.make_async_copy(
                o_buf.at[u, pl.ds(0, tokens)], out_ref.at[:, pl.ds(column, BLOCK)], o_sem.at[0, u]
            )
        ]
        if other_ref is not None:
            at = other_first + u * BLOCK
            at = at if isinstance(u, int) else pl.multiple_of(at, BLOCK)
            copies.append(
                pltpu.make_async_copy(
                    o_buf.at[u, pl.ds(tokens, tokens)],
                    other_ref.at[:, pl.ds(at, BLOCK)],
                    o_sem.at[1, u],
                )
            )
        return copies

    def step(t, width):
        for h in range(width):
            pltpu.make_async_copy(
                w_refs[0].at[pl.ds(0, BLOCK)],
                w_buf.at[pl.ds((t + h) * BLOCK, BLOCK)],
                w_sem.at[t + h],
            ).wait()
        size = width * BLOCK
        start = t * BLOCK if isinstance(t, int) else pl.multiple_of(t * BLOCK, BLOCK)
        total = dot_nt(up_buf[...], w_buf[pl.ds(start, size)])
        acc[:, :size] = total
        for h in range(width):
            o_buf[t + h] = total[:, h * BLOCK : (h + 1) * BLOCK].astype(o_buf.dtype)
        for h in range(width):
            first_b = head[table[t + h]]

            @pl.when(first_b >= 0)
            def _():
                def add(b):
                    column = pl.multiple_of(cols_ref[b] * BLOCK, BLOCK)
                    delta = d_buf[delta_at(slots_ref[b])]
                    acc[:, h * BLOCK : (h + 1) * BLOCK] += dot_nt(
                        up_buf[:, pl.ds(column, BLOCK)], delta
                    )
                    return after_it[b]

                lax.while_loop(lambda b: b >= 0, add, first_b)
                o_buf[t + h] = acc[:, h * BLOCK : (h + 1) * BLOCK].astype(o_buf.dtype)

        for h in range(width):
            for copy in out_copies(t + h):
                copy.start()

    whole = n_units // tile
    if whole > 1:

        def body(k, carry):
            step(k * tile, tile)
            return carry

        lax.fori_loop(0, whole, body, 0)
    elif whole == 1:
        step(0, tile)
    if n_units % tile:
        step(whole * tile, n_units % tile)

    for copy in m_in:
        copy.wait()
    for copy in m_out:
        copy.start()
    for copy in m_out:
        copy.wait()
    for u in range(n_units):
        for copy in out_copies(u):
            copy.wait()


def rows_grad(
    units, weights, rows, cols, slots, ups, deltas, delta_at, width, out=None, moves=(), moved=(), tile=4,
    other=None, other_units=None, other_first=0, vmem=VMEM_BYTES,
):
    n_units = len(units)
    tile = min(tile, n_units)
    tokens, depth = ups[0].shape
    dtype = ups[0].dtype
    stored = sum(d.shape[0] for d in deltas)
    nb = rows.shape[0]
    operands = [rows, cols, slots, *ups, *weights, *deltas, *moved]
    specs = [HBM_SPEC] * 3 + [ANY_SPEC] * (len(operands) - 3)
    alias = {}
    for n, held in enumerate([out, other]):
        if held is not None:
            alias[len(operands)] = n
            operands.append(held)
            specs.append(HBM_SPEC)
    shapes = [jax.ShapeDtypeStruct((tokens, width), dtype)]
    if len(ups) > 1:
        shapes.append(
            jax.ShapeDtypeStruct((tokens, (other_units or n_units) * BLOCK), dtype)
        )
    return pl.pallas_call(
        functools.partial(
            rows_kernel, units, moves, tile, width // BLOCK, delta_at, len(ups), len(weights),
            len(deltas), len(moved), len(alias), other_first,
        ),
        out_shape=shapes,
        in_specs=specs,
        out_specs=[HBM_SPEC] * len(shapes),
        input_output_aliases=alias,
        scratch_shapes=[
            pltpu.SMEM((nb,), jnp.int32),
            pltpu.SMEM((nb,), jnp.int32),
            pltpu.SMEM((nb,), jnp.int32),
            pltpu.VMEM((len(ups) * tokens, depth), dtype),
            pltpu.VMEM((n_units * BLOCK, depth), dtype),
            pltpu.VMEM((stored, BLOCK, BLOCK), dtype),
            pltpu.VMEM((len(ups) * tokens, tile * BLOCK), jnp.float32),
            pltpu.VMEM((n_units, len(ups) * tokens, BLOCK), dtype),
            pltpu.VMEM((max(1, len(moves)), tokens, BLOCK), dtype),
            pltpu.SMEM((n_units,), jnp.int32),
            pltpu.SMEM((width // BLOCK,), jnp.int32),
            pltpu.SMEM((nb,), jnp.int32),
            pltpu.SemaphoreType.DMA((3,)),
            pltpu.SemaphoreType.DMA((len(ups),)),
            pltpu.SemaphoreType.DMA((n_units,)),
            pltpu.SemaphoreType.DMA((len(deltas),)),
            pltpu.SemaphoreType.DMA((len(ups), n_units)),
            pltpu.SemaphoreType.DMA((2, max(1, len(moves)))),
        ],
        compiler_params=pltpu.CompilerParams(vmem_limit_bytes=vmem),
        cost_estimate=COST,
        name="rows_grad",
    )(*operands)


def gathered(activations, upstream, frozen, deltas, block_rows, block_cols, block_slot):
    local_slots = deltas.shape[0]
    n = lax.axis_size("fsdp")
    width = activations.shape[1]
    pattern = (block_rows, block_cols, block_slot)

    (partial,) = block_grads(
        lambda slot: slot, [n * local_slots], *pattern, activations, upstream
    )
    mine = lax.psum_scatter(partial, "fsdp", scatter_dimension=0, tiled=True)
    totals = lax.psum(mine, "dp")

    all_deltas = lax.all_gather(deltas, "fsdp", axis=0, tiled=True)
    weight = lax.all_gather(frozen, "fsdp", axis=0, tiled=True)
    out = None
    for first in range(0, width, 2048):
        units = [
            (0, first + k * BLOCK, lambda c=first // BLOCK + k: c)
            for k in range(min(2048, width - first) // BLOCK)
        ]
        (out,) = rows_grad(
            units, [weight], *pattern, [upstream], [all_deltas], lambda slot: slot, width, out
        )
    tokens = upstream.shape[0] * n * lax.axis_size("dp")
    return out, totals * (1.0 / math.sqrt(tokens))


def relayed(activations, upstream, frozen, deltas, block_rows, block_cols, block_slot):
    local_slots = deltas.shape[0]
    quarter = frozen.shape[0]
    width = activations.shape[1]
    n_dp = lax.axis_size("dp")
    pattern = (block_rows, block_cols, block_slot)

    def my_f():
        return lax.axis_index("fsdp")

    def my_cell():
        return 2 * lax.axis_index("group") + lax.axis_index("dp") % 2

    def over_core(a):
        return lax.ppermute(a, "fsdp", [(k, k ^ 1) for k in range(4)])

    def over_x(a):
        return lax.ppermute(a, "fsdp", [(k, k ^ 2) for k in range(4)])

    def over_y(a):
        return lax.ppermute(a, "group", [(k, k ^ 1) for k in range(2)])

    def over_z(a, step=1):
        return lax.ppermute(a, "dp", [(k, k ^ step) for k in range(n_dp)])

    part = quarter // 4
    sizes = (part // 4, part // 4, part // 2)
    offs = (0, sizes[0], sizes[0] + sizes[1])

    def row_of(flip, k):
        return lambda: (my_cell() ^ flip) * part + offs[k]

    def delta_at(slot):
        return ((slot // local_slots) ^ my_f()) * local_slots + slot % local_slots

    def column_of(flip_f, flip_cell, at):
        def column():
            base = (my_f() ^ flip_f) * (quarter // BLOCK) + at // BLOCK
            if flip_cell is not None:
                base = base + (my_cell() ^ flip_cell) * (part // BLOCK)
            return base

        return column

    def units_of(pieces):
        return [
            (w, k * BLOCK, column_of(flip_f, flip_cell, first + k * BLOCK))
            for w, (a, flip_f, flip_cell, first) in enumerate(pieces)
            for k in range(a.shape[0] // BLOCK)
        ]

    def moves_of(pieces):
        units = [
            (flip_f ^ 1, flip_cell, first + k * BLOCK)
            for a, flip_f, flip_cell, first in pieces
            for k in range(a.shape[0] // BLOCK)
        ]
        return [(0, u * BLOCK, column_of(*unit)) for u, unit in enumerate(units)]

    half = local_slots // 2

    def place(slot):
        rel = (slot // local_slots) ^ my_f()
        at = slot % local_slots
        index = ((at // half) ^ (lax.axis_index("dp") % 2)) * half + at % half
        return ((rel % 2) * 2 + rel // 2) * local_slots + index

    x0 = over_x(lax.dynamic_slice_in_dim(frozen, my_cell() * part, sizes[0], 0))
    up_sib = over_core(upstream)
    dc = over_core(deltas)
    dx = over_x(deltas)
    keep, send, s1, s2, s3 = block_grads(
        place, [2 * local_slots, 2 * local_slots], *pattern, activations, upstream, frozen,
        [(row_of(0, 1), sizes[1]), (row_of(0, 2), sizes[2]), (row_of(3, 1), sizes[1] + sizes[2])],
    )

    x0, send, up_sib, s1, s2, dc = lax.optimization_barrier((x0, send, up_sib, s1, s2, dc))
    y0, z0, x1 = over_y(x0), over_z(x0), over_x(s1)
    gc = over_core(send)
    gx = over_x(keep[local_slots:] + gc[local_slots:])

    dxc = over_core(dx)
    all_deltas = [deltas, dc, dx, dxc]

    def multiply(pieces, ups, out, at=(), moved=(), units=None, **other):
        moves = [
            (m, u * BLOCK, column)
            for m, there in enumerate(at)
            for u, (_, _, column) in enumerate(sum([moves_of(p) for p in there], []))
        ]
        return rows_grad(
            units or units_of(pieces), [p[0] for p in pieces], *pattern, ups, all_deltas, delta_at,
            width, out, moves, moved, **other,
        )

    pieces1 = [(frozen, 0, None, 0)]
    units1 = units_of(pieces1)
    first_half = len(units1) // 2
    n_1 = len(units1) + (2 * sizes[0] + sizes[0] + sizes[1]) // BLOCK
    out, other1 = multiply(
        pieces1, [upstream, after(up_sib, x0)], None, units=units1[:first_half], other_units=n_1
    )

    gx, s2, out, other1, x1 = lax.optimization_barrier((gx, s2, out, other1, x1))
    y0, z0 = lax.optimization_barrier((y0, z0))
    x2 = over_x(s2)
    y1, z1, yd = over_y(x1), over_z(x1), over_y(z0)
    owned = keep[:local_slots] + gc[:local_slots] + gx
    gz = over_z(owned[half:])
    out, other1 = multiply(
        pieces1, [upstream, after(up_sib, x1)], out, units=units1[first_half:],
        other=other1, other_units=n_1, other_first=first_half * BLOCK,
    )
    pieces2 = [(x0, 2, 0, offs[0]), (y0, 2, 2, offs[0]), (z0, 2, 1, offs[0]), (x1, 2, 0, offs[1])]
    out, other1 = multiply(
        pieces2, [upstream, after(up_sib, x1)], out,
        other=other1, other_units=n_1, other_first=len(units1) * BLOCK,
    )

    out, other1, gz, x2, y1, z1, yd = lax.optimization_barrier(
        (out, other1, gz, x2, y1, z1, yd)
    )
    y2, z2 = over_y(x2), over_z(x2)
    x3 = over_x(after(s3, x2))
    mine = owned[:half] + gz
    gz2 = over_z(mine, 2)
    o1 = over_core(other1)
    pieces3 = [
        (y1, 2, 2, offs[1]), (z1, 2, 1, offs[1]), (yd, 2, 3, offs[0]), (x2, 2, 0, offs[2]),
    ]
    out, other2 = multiply(
        pieces3, [upstream, after(up_sib, x2)], out, [[pieces1, pieces2]], [o1]
    )

    out, other2, x3, y2, z2, gz2 = lax.optimization_barrier((out, other2, x3, y2, z2, gz2))
    mine = mine + gz2
    other_half = over_z(mine)
    o2 = over_core(other2)
    last = [(x3, 2, 3, offs[1]), (y2, 2, 2, offs[2]), (z2, 2, 1, offs[2])]
    last = last + [(over_core(a), 3, cell, at) for a, _, cell, at in last]
    (out,) = multiply(last, [upstream], out, [[pieces3]], [o2])
    other_half = after(other_half, out)
    normalizer = 1.0 / math.sqrt(upstream.shape[0] * lax.axis_size("fsdp") * n_dp)
    totals = jnp.where(
        lax.axis_index("dp") % 2 == 0,
        jnp.concatenate([mine, other_half], axis=0),
        jnp.concatenate([other_half, mine], axis=0),
    ) * normalizer
    return out, totals


def solution(mesh):
    sizes = dict(mesh.shape)
    cells = sizes["fsdp"] == 4 and sizes["group"] == 2 and sizes["dp"] == 4
    return jax.shard_map(
        relayed if cells else gathered,
        mesh=mesh,
        in_specs=(
            P(("group", "fsdp", "dp"), None),
            P(("group", "fsdp", "dp"), None),
            P("fsdp", None),
            P(("group", "fsdp"), None, None),
            P(),
            P(),
            P(),
        ),
        out_specs=(P(("group", "fsdp", "dp"), None), P(("group", "fsdp"), None, None)),
        check_vma=False,
    )
```

```python
import functools
import math

import jax
import jax.numpy as jnp
from jax import lax
from jax.experimental import pallas as pl
from jax.experimental.pallas import tpu as pltpu
from jax.sharding import PartitionSpec as P

BLOCK = 128
VMEM_BYTES = 48 * 1024 * 1024
GRAD_VMEM_BYTES = 60 * 1024 * 1024
ANY_SPEC = pl.BlockSpec(memory_space=pl.ANY)
HBM_SPEC = pl.BlockSpec(memory_space=pltpu.HBM)
COST = pl.CostEstimate(flops=1024, bytes_accessed=1024, transcendentals=0)
VMEM_SPEC = pl.BlockSpec(memory_space=pltpu.VMEM)


def dot_nt(left, right):
    return lax.dot_general(
        left, right, (((1,), (1,)), ((), ())), preferred_element_type=jnp.float32
    )


def dot_tn(left, right):
    return lax.dot_general(
        left, right, (((0,), (0,)), ((), ())), preferred_element_type=jnp.float32
    )


def after(value, *earlier):
    return lax.optimization_barrier((value, *earlier))[0]


def grad_kernel(place, outs, cuts, rows_hbm, cols_hbm, slots_hbm, act_ref, up_ref, *refs):
    refs = list(refs)
    w_ref = refs.pop(0) if cuts else None
    out_refs, refs = refs[:outs], refs[outs:]
    cut_refs, refs = refs[: len(cuts)], refs[len(cuts) :]
    rows_ref, cols_ref, slots_ref, act_buf, up_buf, sums, *sems = refs
    act_sem, up_sem, i_sem, c_sem, o_sem = sems
    nb = rows_ref.shape[0]
    index_copies = [
        pltpu.make_async_copy(src, dst, i_sem.at[n])
        for n, (src, dst) in enumerate(
            [(rows_hbm, rows_ref), (cols_hbm, cols_ref), (slots_hbm, slots_ref)]
        )
    ]
    for copy in index_copies:
        copy.start()
    up_copy = pltpu.make_async_copy(up_ref, up_buf, up_sem)
    up_copy.start()

    def act_copy(b):
        column = pl.multiple_of(rows_ref[b] * BLOCK, BLOCK)
        return pltpu.make_async_copy(
            act_ref.at[:, pl.ds(column, BLOCK)], act_buf.at[b], act_sem.at[b]
        )

    for copy in index_copies:
        copy.wait()
    for b in range(nb):
        act_copy(b).start()
    cut_copies = [
        pltpu.make_async_copy(
            w_ref.at[pl.ds(pl.multiple_of(first(), BLOCK), ref.shape[0])], ref, c_sem.at[n]
        )
        for n, ((first, _), ref) in enumerate(zip(cuts, cut_refs))
    ]
    for copy in cut_copies:
        copy.start()
    if sums.shape[0] != nb:
        sums[...] = jnp.zeros_like(sums)
    up_copy.wait()
    for b in range(nb):
        act_copy(b).wait()
    for b in range(nb):
        column = pl.multiple_of(cols_ref[b] * BLOCK, BLOCK)
        sums[place(slots_ref[b])] = dot_tn(act_buf[b], up_buf[:, pl.ds(column, BLOCK)])
    first = 0
    out_copies = []
    for n, ref in enumerate(out_refs):
        out_copies.append(
            pltpu.make_async_copy(sums.at[pl.ds(first, ref.shape[0])], ref, o_sem.at[n])
        )
        first += ref.shape[0]
    for copy in out_copies:
        copy.start()
    for copy in out_copies:
        copy.wait()
    for copy in cut_copies:
        copy.wait()


def block_grads(place, shapes, rows, cols, slots, act, up, weight=None, cuts=()):
    nb = rows.shape[0]
    return pl.pallas_call(
        functools.partial(grad_kernel, place, len(shapes), cuts),
        out_shape=[jax.ShapeDtypeStruct((n, BLOCK, BLOCK), jnp.float32) for n in shapes]
        + [jax.ShapeDtypeStruct((n, weight.shape[1]), weight.dtype) for _, n in cuts],
        in_specs=[HBM_SPEC] * (6 if cuts else 5),
        out_specs=[HBM_SPEC] * len(shapes) + [VMEM_SPEC] * len(cuts),
        scratch_shapes=[
            pltpu.SMEM((nb,), jnp.int32),
            pltpu.SMEM((nb,), jnp.int32),
            pltpu.SMEM((nb,), jnp.int32),
            pltpu.VMEM((nb, act.shape[0], BLOCK), act.dtype),
            pltpu.VMEM(up.shape, up.dtype),
            pltpu.VMEM((sum(shapes), BLOCK, BLOCK), jnp.float32),
            pltpu.SemaphoreType.DMA((nb,)),
            pltpu.SemaphoreType.DMA,
            pltpu.SemaphoreType.DMA((3,)),
            pltpu.SemaphoreType.DMA((max(1, len(cuts)),)),
            pltpu.SemaphoreType.DMA((len(shapes),)),
        ],
        compiler_params=pltpu.CompilerParams(vmem_limit_bytes=GRAD_VMEM_BYTES),
        cost_estimate=COST,
        name="block_grads",
    )(rows, cols, slots, act, up, *([weight] if cuts else []))


def rows_kernel(
    units, moves, tile, row_blocks, delta_at, n_up, n_w, n_d, n_m, n_alias, other_first, *refs
):
    refs = list(refs)

    def take(n):
        taken = refs[:n]
        del refs[:n]
        return taken

    rows_hbm, cols_hbm, slots_hbm = take(3)
    up_refs, w_refs, d_refs, m_refs = take(n_up), take(n_w), take(n_d), take(n_m)
    take(n_alias)
    (out_ref,) = take(1)
    other_ref = take(1)[0] if n_up > 1 else None
    rows_ref, cols_ref, slots_ref, up_buf, w_buf, d_buf, acc, o_buf, m_buf = take(9)
    table, head, after_it, i_sem, up_sem, w_sem, d_sem, o_sem, m_sem = take(9)
    nb = rows_ref.shape[0]
    n_units = len(units)
    per = d_buf.shape[0] // n_d
    tokens = up_buf.shape[0] // n_up

    index_copies = [
        pltpu.make_async_copy(src, dst, i_sem.at[n])
        for n, (src, dst) in enumerate(
            [(rows_hbm, rows_ref), (cols_hbm, cols_ref), (slots_hbm, slots_ref)]
        )
    ]
    for copy in index_copies:
        copy.start()
    up_copies = [
        pltpu.make_async_copy(ref, up_buf.at[pl.ds(n * tokens, tokens)], up_sem.at[n])
        for n, ref in enumerate(up_refs)
    ]
    for copy in up_copies:
        copy.start()
    for u, (w, first, _) in enumerate(units):
        pltpu.make_async_copy(
            w_refs[w].at[pl.ds(first, BLOCK)], w_buf.at[pl.ds(u * BLOCK, BLOCK)], w_sem.at[u]
        ).start()
    d_copies = [
        pltpu.make_async_copy(ref, d_buf.at[pl.ds(n * per, per)], d_sem.at[n])
        for n, ref in enumerate(d_refs)
    ]
    for copy in d_copies:
        copy.start()
    m_in = [
        pltpu.make_async_copy(
            m_refs[m].at[:, pl.ds(first, BLOCK)], m_buf.at[n], m_sem.at[0, n]
        )
        for n, (m, first, _) in enumerate(moves)
    ]
    m_out = [
        pltpu.make_async_copy(
            m_buf.at[n],
            out_ref.at[:, pl.ds(pl.multiple_of(column() * BLOCK, BLOCK), BLOCK)],
            m_sem.at[1, n],
        )
        for n, (_, _, column) in enumerate(moves)
    ]
    for copy in m_in:
        copy.start()
    for u, (_, _, column) in enumerate(units):
        table[u] = column()
    for r in range(row_blocks):
        head[r] = -1
    for copy in index_copies:
        copy.wait()
    for b in range(nb):
        r = rows_ref[b]
        after_it[b] = head[r]
        head[r] = b
    for copy in up_copies:
        copy.wait()
    for copy in d_copies:
        copy.wait()

    def out_copies(u):
        column = pl.multiple_of(table[u] * BLOCK, BLOCK)
        copies = [
            pltpu.make_async_copy(
                o_buf.at[u, pl.ds(0, tokens)], out_ref.at[:, pl.ds(column, BLOCK)], o_sem.at[0, u]
            )
        ]
        if other_ref is not None:
            at = other_first + u * BLOCK
            at = at if isinstance(u, int) else pl.multiple_of(at, BLOCK)
            copies.append(
                pltpu.make_async_copy(
                    o_buf.at[u, pl.ds(tokens, tokens)],
                    other_ref.at[:, pl.ds(at, BLOCK)],
                    o_sem.at[1, u],
                )
            )
        return copies

    def step(t, width):
        for h in range(width):
            pltpu.make_async_copy(
                w_refs[0].at[pl.ds(0, BLOCK)],
                w_buf.at[pl.ds((t + h) * BLOCK, BLOCK)],
                w_sem.at[t + h],
            ).wait()
        size = width * BLOCK
        start = t * BLOCK if isinstance(t, int) else pl.multiple_of(t * BLOCK, BLOCK)
        total = dot_nt(up_buf[...], w_buf[pl.ds(start, size)])
        acc[:, :size] = total
        for h in range(width):
            o_buf[t + h] = total[:, h * BLOCK : (h + 1) * BLOCK].astype(o_buf.dtype)
        for h in range(width):
            first_b = head[table[t + h]]

            @pl.when(first_b >= 0)
            def _():
                def add(b):
                    column = pl.multiple_of(cols_ref[b] * BLOCK, BLOCK)
                    delta = d_buf[delta_at(slots_ref[b])]
                    acc[:, h * BLOCK : (h + 1) * BLOCK] += dot_nt(
                        up_buf[:, pl.ds(column, BLOCK)], delta
                    )
                    return after_it[b]

                lax.while_loop(lambda b: b >= 0, add, first_b)
                o_buf[t + h] = acc[:, h * BLOCK : (h + 1) * BLOCK].astype(o_buf.dtype)

        for h in range(width):
            for copy in out_copies(t + h):
                copy.start()

    whole = n_units // tile
    if whole > 1:

        def body(k, carry):
            step(k * tile, tile)
            return carry

        lax.fori_loop(0, whole, body, 0)
    elif whole == 1:
        step(0, tile)
    if n_units % tile:
        step(whole * tile, n_units % tile)

    for copy in m_in:
        copy.wait()
    for copy in m_out:
        copy.start()
    for copy in m_out:
        copy.wait()
    for u in range(n_units):
        for copy in out_copies(u):
            copy.wait()


def rows_grad(
    units, weights, rows, cols, slots, ups, deltas, delta_at, width, out=None, moves=(), moved=(), tile=8,
    other=None, other_units=None, other_first=0, vmem=VMEM_BYTES,
):
    n_units = len(units)
    tile = min(tile, n_units)
    tokens, depth = ups[0].shape
    dtype = ups[0].dtype
    stored = sum(d.shape[0] for d in deltas)
    nb = rows.shape[0]
    operands = [rows, cols, slots, *ups, *weights, *deltas, *moved]
    specs = [HBM_SPEC] * 3 + [ANY_SPEC] * (len(operands) - 3)
    alias = {}
    for n, held in enumerate([out, other]):
        if held is not None:
            alias[len(operands)] = n
            operands.append(held)
            specs.append(HBM_SPEC)
    shapes = [jax.ShapeDtypeStruct((tokens, width), dtype)]
    if len(ups) > 1:
        shapes.append(
            jax.ShapeDtypeStruct((tokens, (other_units or n_units) * BLOCK), dtype)
        )
    return pl.pallas_call(
        functools.partial(
            rows_kernel, units, moves, tile, width // BLOCK, delta_at, len(ups), len(weights),
            len(deltas), len(moved), len(alias), other_first,
        ),
        out_shape=shapes,
        in_specs=specs,
        out_specs=[HBM_SPEC] * len(shapes),
        input_output_aliases=alias,
        scratch_shapes=[
            pltpu.SMEM((nb,), jnp.int32),
            pltpu.SMEM((nb,), jnp.int32),
            pltpu.SMEM((nb,), jnp.int32),
            pltpu.VMEM((len(ups) * tokens, depth), dtype),
            pltpu.VMEM((n_units * BLOCK, depth), dtype),
            pltpu.VMEM((stored, BLOCK, BLOCK), dtype),
            pltpu.VMEM((len(ups) * tokens, tile * BLOCK), jnp.float32),
            pltpu.VMEM((n_units, len(ups) * tokens, BLOCK), dtype),
            pltpu.VMEM((max(1, len(moves)), tokens, BLOCK), dtype),
            pltpu.SMEM((n_units,), jnp.int32),
            pltpu.SMEM((width // BLOCK,), jnp.int32),
            pltpu.SMEM((nb,), jnp.int32),
            pltpu.SemaphoreType.DMA((3,)),
            pltpu.SemaphoreType.DMA((len(ups),)),
            pltpu.SemaphoreType.DMA((n_units,)),
            pltpu.SemaphoreType.DMA((len(deltas),)),
            pltpu.SemaphoreType.DMA((len(ups), n_units)),
            pltpu.SemaphoreType.DMA((2, max(1, len(moves)))),
        ],
        compiler_params=pltpu.CompilerParams(vmem_limit_bytes=vmem),
        cost_estimate=COST,
        name="rows_grad",
    )(*operands)


def gathered(activations, upstream, frozen, deltas, block_rows, block_cols, block_slot):
    local_slots = deltas.shape[0]
    n = lax.axis_size("fsdp")
    width = activations.shape[1]
    pattern = (block_rows, block_cols, block_slot)

    (partial,) = block_grads(
        lambda slot: slot, [n * local_slots], *pattern, activations, upstream
    )
    mine = lax.psum_scatter(partial, "fsdp", scatter_dimension=0, tiled=True)
    totals = lax.psum(mine, "dp")

    all_deltas = lax.all_gather(deltas, "fsdp", axis=0, tiled=True)
    weight = lax.all_gather(frozen, "fsdp", axis=0, tiled=True)
    out = None
    for first in range(0, width, 2048):
        units = [
            (0, first + k * BLOCK, lambda c=first // BLOCK + k: c)
            for k in range(min(2048, width - first) // BLOCK)
        ]
        (out,) = rows_grad(
            units, [weight], *pattern, [upstream], [all_deltas], lambda slot: slot, width, out
        )
    tokens = upstream.shape[0] * n * lax.axis_size("dp")
    return out, totals * (1.0 / math.sqrt(tokens))


def relayed(activations, upstream, frozen, deltas, block_rows, block_cols, block_slot):
    local_slots = deltas.shape[0]
    quarter = frozen.shape[0]
    width = activations.shape[1]
    n_dp = lax.axis_size("dp")
    pattern = (block_rows, block_cols, block_slot)

    def my_f():
        return lax.axis_index("fsdp")

    def my_cell():
        return 2 * lax.axis_index("group") + lax.axis_index("dp") % 2

    def over_core(a):
        return lax.ppermute(a, "fsdp", [(k, k ^ 1) for k in range(4)])

    def over_x(a):
        return lax.ppermute(a, "fsdp", [(k, k ^ 2) for k in range(4)])

    def over_y(a):
        return lax.ppermute(a, "group", [(k, k ^ 1) for k in range(2)])

    def over_z(a, step=1):
        return lax.ppermute(a, "dp", [(k, k ^ step) for k in range(n_dp)])

    part = quarter // 4
    sizes = (part // 4, part // 4, part // 2)
    offs = (0, sizes[0], sizes[0] + sizes[1])

    def row_of(flip, k):
        return lambda: (my_cell() ^ flip) * part + offs[k]

    def delta_at(slot):
        return ((slot // local_slots) ^ my_f()) * local_slots + slot % local_slots

    def column_of(flip_f, flip_cell, at):
        def column():
            base = (my_f() ^ flip_f) * (quarter // BLOCK) + at // BLOCK
            if flip_cell is not None:
                base = base + (my_cell() ^ flip_cell) * (part // BLOCK)
            return base

        return column

    def units_of(pieces):
        return [
            (w, k * BLOCK, column_of(flip_f, flip_cell, first + k * BLOCK))
            for w, (a, flip_f, flip_cell, first) in enumerate(pieces)
            for k in range(a.shape[0] // BLOCK)
        ]

    def moves_of(pieces):
        units = [
            (flip_f ^ 1, flip_cell, first + k * BLOCK)
            for a, flip_f, flip_cell, first in pieces
            for k in range(a.shape[0] // BLOCK)
        ]
        return [(0, u * BLOCK, column_of(*unit)) for u, unit in enumerate(units)]

    half = local_slots // 2

    def place(slot):
        rel = (slot // local_slots) ^ my_f()
        at = slot % local_slots
        index = ((at // half) ^ (lax.axis_index("dp") % 2)) * half + at % half
        return ((rel % 2) * 2 + rel // 2) * local_slots + index

    x0 = over_x(lax.dynamic_slice_in_dim(frozen, my_cell() * part, sizes[0], 0))
    up_sib = over_core(upstream)
    dc = over_core(deltas)
    dx = over_x(deltas)
    keep, send, s1, s2, s3 = block_grads(
        place, [2 * local_slots, 2 * local_slots], *pattern, activations, upstream, frozen,
        [(row_of(0, 1), sizes[1]), (row_of(0, 2), sizes[2]), (row_of(3, 1), sizes[1] + sizes[2])],
    )

    x0, send, up_sib, s1, s2, dc = lax.optimization_barrier((x0, send, up_sib, s1, s2, dc))
    y0, z0, x1 = over_y(x0), over_z(x0), over_x(s1)
    gc = over_core(send)
    gx = over_x(keep[local_slots:] + gc[local_slots:])

    dxc = over_core(dx)
    all_deltas = [deltas, dc, dx, dxc]

    def multiply(pieces, ups, out, at=(), moved=(), units=None, **other):
        moves = [
            (m, u * BLOCK, column)
            for m, there in enumerate(at)
            for u, (_, _, column) in enumerate(sum([moves_of(p) for p in there], []))
        ]
        return rows_grad(
            units or units_of(pieces), [p[0] for p in pieces], *pattern, ups, all_deltas, delta_at,
            width, out, moves, moved, **other,
        )

    pieces1 = [(frozen, 0, None, 0)]
    units1 = units_of(pieces1)
    first_half = len(units1) // 2
    n_1 = len(units1) + (2 * sizes[0] + sizes[0] + sizes[1]) // BLOCK
    out, other1 = multiply(
        pieces1, [upstream, after(up_sib, x0)], None, units=units1[:first_half], other_units=n_1
    )

    gx, s2, out, other1, x1 = lax.optimization_barrier((gx, s2, out, other1, x1))
    y0, z0 = lax.optimization_barrier((y0, z0))
    x2 = over_x(s2)
    y1, z1, yd = over_y(x1), over_z(x1), over_y(z0)
    owned = keep[:local_slots] + gc[:local_slots] + gx
    gz = over_z(owned[half:])
    out, other1 = multiply(
        pieces1, [upstream, after(up_sib, x1)], out, units=units1[first_half:],
        other=other1, other_units=n_1, other_first=first_half * BLOCK,
    )
    pieces2 = [(x0, 2, 0, offs[0]), (y0, 2, 2, offs[0]), (z0, 2, 1, offs[0]), (x1, 2, 0, offs[1])]
    out, other1 = multiply(
        pieces2, [upstream, after(up_sib, x1)], out,
        other=other1, other_units=n_1, other_first=len(units1) * BLOCK,
    )

    out, other1, gz, x2, y1, z1, yd = lax.optimization_barrier(
        (out, other1, gz, x2, y1, z1, yd)
    )
    y2, z2 = over_y(x2), over_z(x2)
    x3 = over_x(after(s3, x2))
    mine = owned[:half] + gz
    gz2 = over_z(mine, 2)
    o1 = over_core(other1)
    pieces3 = [
        (y1, 2, 2, offs[1]), (z1, 2, 1, offs[1]), (yd, 2, 3, offs[0]), (x2, 2, 0, offs[2]),
    ]
    out, other2 = multiply(
        pieces3, [upstream, after(up_sib, x2)], out, [[pieces1, pieces2]], [o1]
    )

    out, other2, x3, y2, z2, gz2 = lax.optimization_barrier((out, other2, x3, y2, z2, gz2))
    mine = mine + gz2
    other_half = over_z(mine)
    o2 = over_core(other2)
    last = [(x3, 2, 3, offs[1]), (y2, 2, 2, offs[2]), (z2, 2, 1, offs[2])]
    last = last + [(over_core(a), 3, cell, at) for a, _, cell, at in last]
    (out,) = multiply(last, [upstream], out, [[pieces3]], [o2])
    other_half = after(other_half, out)
    normalizer = 1.0 / math.sqrt(upstream.shape[0] * lax.axis_size("fsdp") * n_dp)
    totals = jnp.where(
        lax.axis_index("dp") % 2 == 0,
        jnp.concatenate([mine, other_half], axis=0),
        jnp.concatenate([other_half, mine], axis=0),
    ) * normalizer
    return out, totals


def solution(mesh):
    sizes = dict(mesh.shape)
    cells = sizes["fsdp"] == 4 and sizes["group"] == 2 and sizes["dp"] == 4
    return jax.shard_map(
        relayed if cells else gathered,
        mesh=mesh,
        in_specs=(
            P(("group", "fsdp", "dp"), None),
            P(("group", "fsdp", "dp"), None),
            P("fsdp", None),
            P(("group", "fsdp"), None, None),
            P(),
            P(),
            P(),
        ),
        out_specs=(P(("group", "fsdp", "dp"), None), P(("group", "fsdp"), None, None)),
        check_vma=False,
    )
```
